128 devices in a mesh: mem: 32 (over z, x, core), tile: 4 (over y).
Axes of the slice: x: 4, y: 4, z: 4, core: 2. Of those that a mesh axis runs over, the one named last changes fastest.
Arguments:
- background: float32 [2048, 8192], P('tile', 'mem'), may hold values from -21 to 21
- obs_value: float32 [2048, 128], P('tile', 'mem'), may hold values from -6 to 6
- obs_height: float32 [2048, 128], P('tile', 'mem'), may hold values from 0 to 63
- obs_weight: float32 [2048, 128], P('tile', 'mem'), may hold values from 0.25 to 2
- counts: int32 [2048], P('tile'), may hold values from 1 to 128
- owner: int32 [2048, 1], P('tile'), may hold values from 0 to 127; in each aligned block of 512 rows (0 to 511, 512 to 1023, ...) at most 8 rows name the same one
- loc_index: int32 [2048, 128], P('tile', 'mem'), may hold values from 0 to 15
- loc_table: float32 [16], replicated, may hold values from 0.05 to 1
Outputs:
- analysis: float32 [2048, 8192], P('tile', 'mem')
- owner_load: float32 [128], P(('mem', 'tile'))
The draws below stay inside these ranges and needn't reach their ends.
Inputs may be any that keep to these rules, and one draw needn't show every extreme that they name: Among the columns of one tile at most 8 name the same owner, a bound that some tile reaches.
All inputs are finite; a program needn't handle non-finite values.
Results may differ from the reference program's by a relative error of at most 0.00023.
Values sent between devices are 32-bit elements; how exact they have to be, the bound alone decides.
A program may use at most 64 MiB of HBM per device.

```python
import math
import jax
import jax.numpy as jnp
import numpy as np
from jax import lax

K = 128
LEV = 64
OBS = 128
LOC_N = 16
NS_ITERS = 5
CAP = 8
OWNERS = 128
COLS_T = 512
COLS = 2048


def draw_background(key, part):
    key = jax.random.fold_in(key, 11)
    values = jax.random.truncated_normal(key, -6.0, 6.0, (COLS, K * LEV), jnp.float32)
    return values.astype(jnp.float32)


def plant(array, key, smallest, high):
    longest = array.shape.index(max(array.shape))
    spots = []
    for shift in (0, 1):
        where = [jax.random.randint(jax.random.fold_in(key, axis), (), 0, length) for axis, length in enumerate(array.shape)]
        where[longest] = (where[longest] + shift) % array.shape[longest]
        spots.append(tuple(where))
    return array.at[spots[0]].set(smallest).at[spots[1]].set(high)


def level_of(key, shape, pieces, low, largest):
    def one(position, blocks):
        draws = jax.random.uniform(jax.random.fold_in(jax.random.fold_in(key, 6), position), (blocks,), jnp.float32, low / len(pieces), largest / len(pieces))
        return jnp.repeat(jnp.exp(draws), shape[position] // blocks).reshape((-1,) + (1,) * (len(shape) - position - 1))

    gain = one(*pieces[0])
    for cut in pieces[1:]:
        gain = gain * one(*cut)
    return gain


def assign_block(key, own, number, rows, number_of, top, limit, skew):
    order = jax.random.permutation(key, number_of)
    heavy_load, ordinary = portions_of(number_of, rows * top, limit, skew, True), portions_of(number_of, rows * top, limit, skew, False)
    places = jnp.arange(number_of)

    def named(tallies, offset_by):
        used = int((tallies > 0).sum())
        fixed = max(1, used // 4)
        shifted = fixed + (places - fixed + offset_by * (used - fixed)) % max(1, number_of - fixed)
        return jnp.zeros((number_of,), jnp.int32).at[order[jnp.where(places < fixed, places, shifted)]].set(jnp.asarray(tallies, jnp.int32))

    tallies = jnp.where(number % 4 == 0, named(heavy_load, number // 4), named(ordinary, number - number // 4 - 1))
    mixed = jax.random.permutation(jax.random.fold_in(own, 3), number_of)
    donor, receiver = mixed[0:number_of // 2 * 2:2], mixed[1:number_of // 2 * 2:2]
    room = jnp.minimum(tallies[donor] - 1, limit - tallies[receiver]) // 2
    room = jnp.where((donor == order[0]) | (receiver == order[0]) | (tallies[receiver] == 0), 0, jnp.maximum(room, 0))
    shifted = jax.random.randint(jax.random.fold_in(own, 4), (number_of // 2,), 0, 1 << 20) % (room + 1)
    tallies = tallies.at[donor].add(-shifted).at[receiver].add(shifted)
    items = jnp.searchsorted(jnp.cumsum(tallies), jnp.arange(rows * top), side="right").astype(jnp.int32)
    listing = items.reshape(top, rows).T
    listing = listing[jax.random.permutation(jax.random.fold_in(own, 1), rows)]
    offset_by = jax.random.randint(jax.random.fold_in(own, 2), (rows, 1), 0, top)
    return jnp.take_along_axis(listing, (jnp.arange(top)[None, :] + offset_by) % top, axis=1)


def portions_of(amount, total, reach, lean, full):
    weights = [(1 << 20) // math.isqrt(rank ** lean) + 1 for rank in range(1, amount + 1)]
    largest = reach if full else min(reach, max(-(-total // amount), total * weights[0] // sum(weights)))
    least = 1 if total - largest >= amount - 1 else 0
    given, surplus = [largest] + [least] * (amount - 1), total - largest - least * (amount - 1)
    while surplus > 0:
        movable = [i for i in range(1, amount) if given[i] < largest] or [i for i in range(1, amount) if given[i] < reach]
        pool, left = sum([weights[i] for i in movable]), surplus
        for i in movable:
            addition = min(reach - given[i], max(1, left * weights[i] // pool), surplus)
            given[i] = given[i] + addition
            surplus = surplus - addition
    return np.array(given)


def scatter_about(key, extent, scale, limit, shards=(), kind=jnp.bfloat16):
    drawn = jax.random.normal(key, extent, jnp.float32) * scale
    if len(shards) > 0:
        drawn = level_of(key, extent, shards, -0.22, 0.18) * drawn
    return jnp.clip(drawn, min=-limit, max=limit).astype(kind)


def setup_inputs(seed: int = 0) -> dict:
    seeds = jax.random.split(jax.random.key(seed), 9)
    background = draw_background(jax.random.fold_in(seeds[8], 71), 0)
    obs_value = scatter_about(seeds[1], (COLS, OBS), 1.0, 6.0, ((0, 4), (1, 32)), jnp.float32)
    obs_height = jnp.clip(63.0 * jax.random.uniform(seeds[2], (COLS, OBS), jnp.float32) ** level_of(seeds[2], (COLS, OBS), ((0, 4), (1, 32)), -0.2, 0.2), 0.0, 63.0)
    obs_weight = jnp.clip(jnp.exp(math.log(2.0) - 2.0794415 * jax.random.uniform(seeds[3], (COLS, OBS), jnp.float32) ** level_of(seeds[3], (COLS, OBS), ((0, 4), (1, 32)), -0.2, 0.2)), 0.25, 2.0)
    counts = plant(jax.random.randint(seeds[4], (COLS,), 1, OBS + 1), jax.random.fold_in(seeds[4], 1), 1, OBS).astype(jnp.int32)
    owner_keys = jax.random.split(jax.random.fold_in(seeds[5], 1), COLS // COLS_T)
    owner_turns = jax.random.permutation(jax.random.fold_in(seeds[5], 3), COLS // COLS_T)
    owner = jax.vmap(lambda own, number: assign_block(jax.random.fold_in(seeds[5], 2), own, number, COLS_T, OWNERS, 1, CAP, 2))(owner_keys, owner_turns).reshape((COLS, 1))
    loc_index = plant(jax.random.randint(seeds[6], (COLS, OBS), 0, LOC_N), jax.random.fold_in(seeds[6], 1), 0, LOC_N - 1).astype(jnp.int32)
    loc_table = jnp.clip(jnp.exp(jax.random.uniform(seeds[7], (LOC_N,), jnp.float32, math.log(0.05), math.log(1.0))), 0.05, 1.0)
    return {"background": background, "obs_value": obs_value, "obs_height": obs_height, "obs_weight": obs_weight, "counts": counts, "owner": owner, "loc_index": loc_index, "loc_table": loc_table}


PRECISE = lax.Precision.HIGHEST

def analyse(states, values, heights, weights):
    members = states.shape[2]
    levels_count = states.shape[1]
    centre = lax.optimization_barrier(jnp.mean(states, axis=2))
    perturb = states - centre[:, :, None]
    level_axis = jnp.arange(levels_count).astype(jnp.float32)
    interp = jnp.maximum(0.0, 1.0 - jnp.abs(level_axis[None, None, :] - heights[:, :, None]))
    obs_pert = jnp.einsum('sol,slk->sok', interp, perturb, precision=PRECISE)
    obs_mean = jnp.einsum('sol,sl->so', interp, centre, precision=PRECISE)
    innovation = values - obs_mean
    weighted = obs_pert * weights[:, :, None]
    identity = jnp.eye(members, dtype=jnp.float32)
    gram_matrix = jnp.einsum('soj,sok->sjk', weighted, obs_pert, precision=PRECISE) + (members - 1.0) * identity
    frobenius = jnp.sqrt(lax.optimization_barrier(jnp.sum(gram_matrix * gram_matrix, axis=(1, 2))))
    root_iter = gram_matrix / frobenius[:, None, None]
    inverse_iter = jnp.broadcast_to(identity, root_iter.shape)
    for sweep_index in range(NS_ITERS):
        middle = 1.5 * identity - 0.5 * jnp.einsum('sij,sjk->sik', inverse_iter, root_iter, precision=PRECISE)
        root_iter, inverse_iter = (jnp.einsum('sij,sjk->sik', root_iter, middle, precision=PRECISE), jnp.einsum('sij,sjk->sik', middle, inverse_iter, precision=PRECISE))
    spread = jnp.sqrt(members - 1.0) * inverse_iter / jnp.sqrt(frobenius)[:, None, None]
    covariance = jnp.einsum('sij,sjk->sik', inverse_iter, inverse_iter, precision=PRECISE) / frobenius[:, None, None]
    forcing = jnp.einsum('sok,so->sk', weighted, innovation, precision=PRECISE)
    mean_weight = jnp.einsum('sjk,sk->sj', covariance, forcing, precision=PRECISE)
    combined = spread + mean_weight[:, :, None]
    return centre[:, :, None] + jnp.einsum('slj,sjk->slk', perturb, combined, precision=PRECISE)

def reference(background, obs_value, obs_height, obs_weight, counts, owner, loc_index, loc_table):
    live_slot = (jnp.arange(OBS).astype(jnp.int32)[None, :] < counts[:, None]).astype(jnp.float32)
    weights = loc_table[loc_index] * obs_weight * live_slot
    states = background.reshape(COLS, K, LEV).transpose(0, 2, 1)
    block_rows = 64
    groups = COLS // block_rows
    blocked = (states.reshape(groups, block_rows, LEV, K), obs_value.reshape(groups, block_rows, OBS), obs_height.reshape(groups, block_rows, OBS), weights.reshape(groups, block_rows, OBS))
    result = lax.map(lambda parts: analyse(parts[0], parts[1], parts[2], parts[3]), blocked)
    analysis = result.reshape(COLS, LEV, K).transpose(0, 2, 1).reshape(COLS, K * LEV)
    column_load = lax.optimization_barrier(jnp.sum(weights, axis=1))
    owner_load = jax.ops.segment_sum(column_load, owner[:, 0], num_segments=OWNERS) / (OBS * CAP)
    return (analysis, owner_load)
```

```python
import functools

import jax
import jax.numpy as jnp
from jax import lax
from jax.experimental import pallas as pl
from jax.experimental.pallas import tpu as pltpu
from jax.sharding import PartitionSpec as P

LEV = 64
OBS = 128
LOC_N = 16
CAP = 8
N_MEM = 32
N_TILE = 4
COLS_T = 512
OWN = COLS_T // N_MEM
CHUNK = 8
CHUNKS = OWN // CHUNK
OBS_L = OBS // N_MEM
WIDTH = 256

F32 = jnp.float32
BF16 = jnp.bfloat16
MESH = pl.DeviceIdType.MESH


def iota(shape, axis):
    return lax.broadcasted_iota(jnp.int32, shape, axis)


def split(x):
    high = x.astype(BF16)
    return high, (x - high.astype(F32)).astype(BF16)


def right_side(x, keep0, keep1):
    high, low = split(x)
    top = jnp.concatenate([high * keep0, low * keep0], 1)
    bottom = jnp.concatenate([high * keep1, low * keep1], 1)
    return jnp.concatenate([top, bottom, top, bottom], 0)


def product(a, right):
    high, low = split(a)
    both = jnp.dot(jnp.concatenate([high, low], 1), right, preferred_element_type=F32)
    return both[:, :128] + both[:, 128:]


def analyse(blocks, values, heights, weights):
    n = len(blocks)
    lane = iota((64, 128), 1)
    row = iota((64, 128), 0)
    left = lane < 64
    left1 = left[:1]
    keep0 = jnp.where(left, 1.0, 0.0).astype(BF16)
    keep1 = jnp.where(left, 0.0, 1.0).astype(BF16)
    eye = jnp.where((lane & 63) == row, 1.0, 0.0)
    eye_left = jnp.where(lane == row, 1.0, 0.0)
    level = row.astype(F32)
    perturb, centre, square, diag, off, force = [], [], [], [], [], []
    for i in range(n):
        x = jnp.concatenate([blocks[i][:, :128], blocks[i][:, 128:]], 0)
        total = jnp.sum(x, 0, keepdims=True)
        mean = (total + pltpu.roll(total, 64, 1)) * (1.0 / 128.0)
        x = x - mean
        high, low = split(x)
        square.append(
            lax.dot_general(
                jnp.concatenate([high, high, low, low], 0),
                jnp.concatenate([high, low, high, low], 0),
                (((0,), (0,)), ((), ())),
                preferred_element_type=F32,
            )
        )
        hat = jnp.maximum(0.0, 1.0 - jnp.abs(level - heights[i]))
        hat_next = jnp.maximum(0.0, 1.0 - jnp.abs((level + 1.0) - heights[i]))
        weighted = weights[i] * hat
        diag.append(jnp.sum(weighted * hat, 1, keepdims=True))
        off.append(jnp.sum(weighted * hat_next, 1, keepdims=True))
        mean_col = jnp.sum(eye_left * mean, 1, keepdims=True)
        innovation = values[i] - jnp.sum(hat * mean_col, 0, keepdims=True)
        force.append(jnp.sum(weighted * innovation, 1, keepdims=True))
        perturb.append(x)
        centre.append(mean)
    base, force_row = [], []
    for i in range(0, n, 2):
        j = i + 1
        g = jnp.where(left, square[i][:64], square[j][64:]) + pltpu.roll(
            jnp.where(left, square[j][:64], square[i][64:]), 64, 1
        )
        d = jnp.where(left, diag[i], diag[j])
        e = jnp.where(left, off[i], off[j])
        w = jnp.where(left, force[i], force[j])
        base.append(d * g + pltpu.roll(e * g, 1, 0) + e * pltpu.roll(g, 63, 0))
        force_row.append(jnp.broadcast_to(jnp.sum(w * g, 0, keepdims=True), (16, 128)))
    y, z, t, inverse = [], [], [], []
    for b, w in zip(base, force_row):
        out = product(jnp.concatenate([b, w], 0), right_side(b, keep0, keep1))
        b2, wb = out[:64], out[64:]
        trace = jnp.sum(eye * (254.0 * b + b2), 0, keepdims=True)
        norm2 = 127.0 * 127.0 * 128.0 + jnp.where(
            left1,
            jnp.sum(jnp.where(left1, trace, 0.0), 1, keepdims=True),
            jnp.sum(jnp.where(left1, 0.0, trace), 1, keepdims=True),
        )
        a = lax.rsqrt(norm2)
        c = (127.0 * eye + b) * a
        c2 = (16129.0 * eye + 254.0 * b + b2) * (a * a)
        y.append(1.5 * c - 0.5 * c2)
        z.append(1.5 * eye - 0.5 * c)
        t.append(1.5 * w - (0.5 * a) * (127.0 * w + wb))
        inverse.append(a)
    pairs = range(len(y))
    for sweep in range(4):
        middle = [
            1.5 * eye - 0.5 * product(z[q], right_side(y[q], keep0, keep1)) for q in pairs
        ]
        for q in pairs:
            right = right_side(middle[q], keep0, keep1)
            if sweep < 3:
                out = product(jnp.concatenate([y[q], z[q], t[q]], 0), right)
                y[q], z[q], t[q] = out[:64], out[64:128], out[128:]
            else:
                out = product(jnp.concatenate([z[q], t[q]], 0), right)
                z[q], t[q] = out[:64], out[64:]
    results = []
    for q in pairs:
        swapped = pltpu.roll(z[q], 64, 1)
        scale = jnp.sqrt(127.0 * inverse[q])
        scale_swapped = pltpu.roll(scale, 64, 1)
        for j in (0, 1):
            i = 2 * q + j
            mine = left if j == 0 else ~left
            mine1 = mine[:1]
            right = right_side(jnp.where(mine, z[q], swapped), keep0, keep1)
            out = product(jnp.concatenate([perturb[i], t[q]], 0), right)
            shift = inverse[q] * out[64:65]
            shift = jnp.where(mine1, shift, pltpu.roll(shift, 64, 1))
            factor = jnp.where(mine1, scale, scale_swapped)
            full = (centre[i] + shift) + factor * out[:64]
            results.append(jnp.concatenate([full[:32], full[32:]], 1))
    return results


def swap_blocks(x):
    row = iota(x.shape, 0)
    block = iota(x.shape, 1) // 16
    for s in (1, 2, 4):
        row_bit = (row // s) % 2
        block_bit = (block // s) % 2
        up = pltpu.roll(pltpu.roll(x, 64 - s, 0), 16 * s, 1)
        down = pltpu.roll(pltpu.roll(x, s, 0), 128 - 16 * s, 1)
        x = jnp.where(row_bit == block_bit, x, jnp.where(row_bit < block_bit, up, down))
    return x


def offsets():
    every = [(z, x, c) for z in range(4) for x in range(4) for c in range(2) if z or x or c]
    return sorted(every, key=lambda o: (-(min(o[0], 4 - o[0]) + min(o[1], 4 - o[1])), o[2]))


def kernel(
    bg, value, height, obs_weight, index, counts, owner, table, out, load_out,
    value_v, height_v, weight_v, index_v, counts_v, owner_v, table_v,
    message, received, fields, load_send, load_recv, rows_in, rows_out,
    small_sem, in_send, in_recv, out_send, out_recv, obs_send, obs_recv, load_sems,
):
    me = lax.axis_index("mem")
    tile = lax.axis_index("tile")
    z, x, core = me // 8, (me // 2) % 4, me % 2
    partners = [
        ((z + dz) % 4) * 8 + ((x + dx) % 4) * 2 + (core + dc) % 2 for dz, dx, dc in offsets()
    ]
    tile_partners = [(tile + d) % N_TILE for d in range(1, N_TILE)]
    small = [
        pltpu.make_async_copy(a, b, small_sem.at[i])
        for i, (a, b) in enumerate(
            zip(
                (value, height, obs_weight, index, counts, owner, table),
                (value_v, height_v, weight_v, index_v, counts_v, owner_v, table_v),
            )
        )
    ]
    for copy in small:
        copy.start()
    barrier = pltpu.get_barrier_semaphore()
    for p in partners:
        pl.semaphore_signal(barrier, inc=1, device_id=(p, tile), device_id_type=MESH)
    for q in tile_partners:
        pl.semaphore_signal(barrier, inc=1, device_id=(me, q), device_id_type=MESH)
    for copy in small:
        copy.wait()

    localised = jnp.zeros((OBS_L, COLS_T), F32)
    entry = index_v[...]
    table_row = table_v[...]
    for k in range(LOC_N):
        localised = jnp.where(entry == k, table_row[:, k : k + 1], localised)
    live = (me * OBS_L + iota((OBS_L, COLS_T), 0)) < counts_v[...]
    weights = jnp.where(live, localised * weight_v[...], 0.0)
    first = jnp.concatenate([value_v[...], height_v[...]], 0)
    second = jnp.concatenate([weights, jnp.zeros((OBS_L, COLS_T), F32)], 0)
    stack = []
    for b in range(4):
        stack += [first[:, 128 * b : 128 * b + 128], second[:, 128 * b : 128 * b + 128]]
    stack = swap_blocks(jnp.concatenate(stack, 0))
    column_load = jnp.sum(weights, 0, keepdims=True)
    right_half = jnp.concatenate([stack[16 * b + 8 : 16 * b + 16] for b in range(4)], 0)
    lane = iota((N_MEM, 128), 1)
    first_owner = iota((N_MEM, COLS_T), 0) * N_TILE
    owners = owner_v[...]
    for q in range(N_TILE):
        part = jnp.sum(
            jnp.where(first_owner + q == owners, column_load, 0.0), 1, keepdims=True
        )
        right_half = jnp.where(lane == 64 + q, part, right_half)
    left_half = jnp.concatenate([stack[16 * b : 16 * b + 8] for b in range(4)], 0)
    message[...] = jnp.concatenate([left_half, right_half], 1).reshape(N_MEM, 1, WIDTH)

    pl.semaphore_wait(barrier, N_MEM - 1 + N_TILE - 1)

    def send_rows(c):
        def source(p):
            return bg.at[pl.ds(pl.multiple_of(p * OWN + c * CHUNK, CHUNK), CHUNK)]

        for p in partners:
            pltpu.make_async_remote_copy(
                src_ref=source(p),
                dst_ref=rows_in.at[c, me],
                send_sem=in_send.at[c],
                recv_sem=in_recv.at[c],
                device_id=(p, tile),
                device_id_type=MESH,
            ).start()
        pltpu.make_async_copy(source(me), rows_in.at[c, me], in_recv.at[c]).start()

    send_rows(0)
    for p in partners:
        pltpu.make_async_remote_copy(
            src_ref=message.at[p],
            dst_ref=received.at[me],
            send_sem=obs_send,
            recv_sem=obs_recv,
            device_id=(p, tile),
            device_id_type=MESH,
        ).start()
    pltpu.make_async_copy(message.at[me], received.at[me], obs_recv).start()
    for c in range(1, CHUNKS):
        send_rows(c)

    pltpu.make_async_copy(received, received, obs_recv).wait()
    arrived = received[...].reshape(N_MEM, WIDTH)
    arrived = jnp.concatenate([arrived, jnp.zeros((128 - N_MEM, WIDTH), F32)], 0).T
    for f in range(3):
        fields[f] = jnp.concatenate(
            [arrived[(4 * f + o) * OWN : (4 * f + o + 1) * OWN, :N_MEM] for o in range(OBS_L)], 1
        )
    loads = jnp.sum(arrived[192 : 192 + N_TILE], 1, keepdims=True)
    load_send[...] = jnp.broadcast_to(loads, (N_TILE, 128)).reshape(N_TILE, 1, 128)
    for q in tile_partners:
        pltpu.make_async_remote_copy(
            src_ref=load_send.at[q],
            dst_ref=load_recv.at[tile],
            send_sem=load_sems.at[0],
            recv_sem=load_sems.at[1],
            device_id=(me, q),
            device_id_type=MESH,
        ).start()
    pltpu.make_async_copy(load_send.at[tile], load_recv.at[tile], load_sems.at[1]).start()

    def step(c, carry):
        pltpu.make_async_copy(rows_in.at[c], rows_in.at[c], in_recv.at[c]).wait()
        base = pl.multiple_of(c * CHUNK, CHUNK)
        obs = [fields[f, pl.ds(base, CHUNK)] for f in range(3)]
        results = analyse(
            [rows_in[c, :, i, :] for i in range(CHUNK)],
            *[[a[i : i + 1] for i in range(CHUNK)] for a in obs],
        )
        for i in range(CHUNK):
            rows_out[c, :, i, :] = results[i]
        target = out.at[pl.ds(pl.multiple_of(me * OWN + c * CHUNK, CHUNK), CHUNK)]
        for p in partners:
            pltpu.make_async_remote_copy(
                src_ref=rows_out.at[c, p],
                dst_ref=target,
                send_sem=out_send.at[c],
                recv_sem=out_recv.at[c],
                device_id=(p, tile),
                device_id_type=MESH,
            ).start()
        pltpu.make_async_copy(rows_out.at[c, me], target, out_recv.at[c]).start()
        return carry

    lax.fori_loop(0, CHUNKS, step, 0)

    pltpu.make_async_copy(load_recv, load_recv, load_sems.at[1]).wait()
    load_out[...] = jnp.sum(load_recv[...], 0)[:, :1] * (1.0 / (OBS * CAP))
    sent = load_send.at[pl.ds(0, N_TILE - 1)]
    pltpu.make_async_copy(sent, sent, load_sems.at[0]).wait()
    sent = message.at[pl.ds(0, N_MEM - 1)]
    pltpu.make_async_copy(sent, sent, obs_send).wait()
    for c in range(CHUNKS):
        sent = rows_in.at[c, pl.ds(0, N_MEM - 1)]
        pltpu.make_async_copy(sent, sent, in_send.at[c]).wait()
        pltpu.make_async_copy(sent, sent, out_send.at[c]).wait()
        pltpu.make_async_copy(rows_out.at[c], rows_out.at[c], out_recv.at[c]).wait()


def per_device(background, obs_value, obs_height, obs_weight, counts, owner, loc_index, loc_table):
    hbm = pl.BlockSpec(memory_space=pl.ANY)
    dma = pltpu.SemaphoreType.DMA
    analysis, load = pl.pallas_call(
        kernel,
        out_shape=(
            jax.ShapeDtypeStruct((COLS_T, WIDTH), F32),
            jax.ShapeDtypeStruct((1, 1), F32),
        ),
        in_specs=[hbm] * 8,
        out_specs=(hbm, pl.BlockSpec(memory_space=pltpu.VMEM)),
        scratch_shapes=[
            pltpu.VMEM((OBS_L, COLS_T), F32),
            pltpu.VMEM((OBS_L, COLS_T), F32),
            pltpu.VMEM((OBS_L, COLS_T), F32),
            pltpu.VMEM((OBS_L, COLS_T), jnp.int32),
            pltpu.VMEM((1, COLS_T), jnp.int32),
            pltpu.VMEM((1, COLS_T), jnp.int32),
            pltpu.VMEM((1, LOC_N), F32),
            pltpu.VMEM((N_MEM, 1, WIDTH), F32),
            pltpu.VMEM((N_MEM, 1, WIDTH), F32),
            pltpu.VMEM((3, OWN, OBS), F32),
            pltpu.VMEM((N_TILE, 1, 128), F32),
            pltpu.VMEM((N_TILE, 1, 128), F32),
            pltpu.VMEM((CHUNKS, N_MEM, CHUNK, WIDTH), F32),
            pltpu.VMEM((CHUNKS, N_MEM, CHUNK, WIDTH), F32),
            dma((7,)),
            dma((CHUNKS,)),
            dma((CHUNKS,)),
            dma((CHUNKS,)),
            dma((CHUNKS,)),
            dma,
            dma,
            dma((2,)),
        ],
        compiler_params=pltpu.CompilerParams(
            collective_id=0, has_side_effects=True, vmem_limit_bytes=60 << 20
        ),
    )(
        background,
        obs_value.T,
        obs_height.T,
        obs_weight.T,
        loc_index.T,
        counts.reshape(1, COLS_T),
        owner.reshape(1, COLS_T),
        loc_table.reshape(1, LOC_N),
    )
    return analysis, load.reshape(1)


def solution(mesh):
    placed = (
        P("tile", "mem"),
        P("tile", "mem"),
        P("tile", "mem"),
        P("tile", "mem"),
        P("tile"),
        P("tile", None),
        P("tile", "mem"),
        P(),
    )
    return jax.shard_map(
        per_device,
        mesh=mesh,
        in_specs=placed,
        out_specs=(P("tile", "mem"), P(("mem", "tile"))),
        check_vma=False,
    )
```

```python
import functools

import jax
import jax.numpy as jnp
from jax import lax
from jax.experimental import pallas as pl
from jax.experimental.pallas import tpu as pltpu
from jax.sharding import PartitionSpec as P

LEV = 64
OBS = 128
LOC_N = 16
CAP = 8
N_MEM = 32
N_TILE = 4
COLS_T = 512
OWN = COLS_T // N_MEM
CHUNK = 8
CHUNKS = OWN // CHUNK
OBS_L = OBS // N_MEM
WIDTH = 256

F32 = jnp.float32
BF16 = jnp.bfloat16
MESH = pl.DeviceIdType.MESH


def iota(shape, axis):
    return lax.broadcasted_iota(jnp.int32, shape, axis)


def split(x):
    high = x.astype(BF16)
    return high, (x - high.astype(F32)).astype(BF16)


def right_side(x, keep0, keep1):
    high, low = split(x)
    top = jnp.concatenate([high * keep0, low * keep0], 1)
    bottom = jnp.concatenate([high * keep1, low * keep1], 1)
    return jnp.concatenate([top, bottom, top, bottom], 0)


def product(a, right):
    high, low = split(a)
    both = jnp.dot(jnp.concatenate([high, low], 1), right, preferred_element_type=F32)
    return both[:, :128] + both[:, 128:]


def lane_masks():
    lane = iota((64, 128), 1)
    left = lane < 64
    keep0 = jnp.where(left, 1.0, 0.0).astype(BF16)
    keep1 = jnp.where(left, 0.0, 1.0).astype(BF16)
    return lane, iota((64, 128), 0), left, keep0, keep1


def observe(fields, shared):
    left = lane_masks()[2]
    level = iota((64, 128), 0).astype(F32)

    def pair(q, carry):
        both = []
        for j in (0, 1):
            value, height, weight = [fields[f, pl.ds(2 * q + j, 1), :] for f in range(3)]
            hat = jnp.maximum(0.0, 1.0 - jnp.abs(level - height))
            hat_next = jnp.maximum(0.0, 1.0 - jnp.abs((level + 1.0) - height))
            weighted = weight * hat
            terms = (weighted * hat, weighted * hat_next, weighted * value)
            both.append([jnp.sum(x, 1, keepdims=True) for x in terms])
        for k in range(3):
            shared[q, k] = jnp.where(left, both[0][k], both[1][k])
        return carry

    lax.fori_loop(0, OWN // 2, pair, 0)


def analyse(blocks, shared):
    lane, row, left, keep0, keep1 = lane_masks()
    left1 = left[:1]
    eye = jnp.where((lane & 63) == row, 1.0, 0.0)
    eye_left = jnp.where(lane == row, 1.0, 0.0)
    pairs = range(len(shared))

    def own(x, j):
        return jnp.where(left[: x.shape[0]] == (j == 0), x, pltpu.roll(x, 64, 1))

    halves, centre, square, mean_col = [], [], [], []
    for block in blocks:
        x = jnp.concatenate([block[:, :128], block[:, 128:]], 0)
        total = jnp.sum(x, 0, keepdims=True)
        mean = (total + pltpu.roll(total, 64, 1)) * (1.0 / 128.0)
        high, low = split(x - mean)
        both = lax.dot_general(
            jnp.concatenate([high, low], 0),
            jnp.concatenate([jnp.concatenate([high, low], 1)] * 2, 0),
            (((0,), (0,)), ((), ())),
            preferred_element_type=F32,
        )
        square.append(both[:, :128] + both[:, 128:])
        mean_col.append(jnp.sum(eye_left * mean, 1, keepdims=True))
        halves.append(jnp.concatenate([high, low], 1))
        centre.append(mean)
    base, force = [], []
    for q in pairs:
        i, j = 2 * q, 2 * q + 1
        g = jnp.where(left, square[i][:64], square[j][64:]) + pltpu.roll(
            jnp.where(left, square[j][:64], square[i][64:]), 64, 1
        )
        d, e, w = shared[q]

        def tridiagonal(m):
            return d * m + pltpu.roll(e * m, 1, 0) + e * pltpu.roll(m, 63, 0)

        w = w - tridiagonal(jnp.where(left, mean_col[i], mean_col[j]))
        base.append(tridiagonal(g))
        force.append(jnp.broadcast_to(jnp.sum(w * g, 0, keepdims=True), (16, 128)))
    right = [right_side(b, keep0, keep1) for b in base]
    out = [product(jnp.concatenate([base[q], force[q]], 0), right[q]) for q in pairs]
    cube = [product(out[q][:64], right[q]) for q in pairs]
    p, z, t, inverse = [], [], [], []
    for q in pairs:
        b, b2 = base[q], out[q][:64]
        trace = jnp.sum(eye * (254.0 * b + b2), 0, keepdims=True)
        norm2 = 127.0 * 127.0 * 128.0 + jnp.where(
            left1,
            jnp.sum(jnp.where(left1, trace, 0.0), 1, keepdims=True),
            jnp.sum(jnp.where(left1, 0.0, trace), 1, keepdims=True),
        )
        a = lax.rsqrt(norm2)
        u = 127.0 * a
        p.append(
            (u * (2.25 + u * (-1.5 + 0.25 * u))) * eye
            + (a * (2.25 + u * (-3.0 + 0.75 * u))) * b
            + (a * a * (-1.5 + 0.75 * u)) * b2
            + (a * a * a * 0.25) * cube[q]
        )
        z.append((1.5 - 0.5 * u) * eye - (0.5 * a) * b)
        t.append((1.5 - 0.5 * u) * force[q] - (0.5 * a) * out[q][64:])
        inverse.append(a)
    for sweep in range(3):
        right = [right_side(p[q], keep0, keep1) for q in pairs]
        out = [product(jnp.concatenate([p[q], z[q], t[q]], 0), right[q]) for q in pairs]
        cube = [product(out[q][:64], right[q]) for q in pairs]
        for q in pairs:
            z[q] = 1.5 * z[q] - 0.5 * out[q][64:128]
            t[q] = 1.5 * t[q] - 0.5 * out[q][128:]
            p[q] = 2.25 * p[q] - 1.5 * out[q][:64] + 0.25 * cube[q]
    results = []
    for q in pairs:
        out = product(jnp.concatenate([z[q], t[q]], 0), right_side(p[q], keep0, keep1))
        z[q] = 1.5 * z[q] - 0.5 * out[:64]
        t[q] = 1.5 * t[q] - 0.5 * out[64:]
    for q in pairs:
        scale = jnp.sqrt(127.0 * inverse[q])
        t_halves = jnp.concatenate(split(t[q]), 1)
        for j in (0, 1):
            i = 2 * q + j
            both = jnp.dot(
                jnp.concatenate([halves[i], t_halves], 0),
                right_side(own(z[q], j), keep0, keep1),
                preferred_element_type=F32,
            )
            both = both[:, :128] + both[:, 128:]
            full = (centre[i] + own(inverse[q] * both[64:65], j)) + own(scale, j) * both[:64]
            results.append(jnp.concatenate([full[:32], full[32:]], 1))
    return results


def swap_blocks(x):
    row = iota(x.shape, 0)
    block = iota(x.shape, 1) // 16
    for s in (1, 2, 4):
        row_bit = (row // s) % 2
        block_bit = (block // s) % 2
        up = pltpu.roll(pltpu.roll(x, 64 - s, 0), 16 * s, 1)
        down = pltpu.roll(pltpu.roll(x, s, 0), 128 - 16 * s, 1)
        x = jnp.where(row_bit == block_bit, x, jnp.where(row_bit < block_bit, up, down))
    return x


def offsets():
    every = [(z, x, c) for z in range(4) for x in range(4) for c in range(2) if z or x or c]
    return sorted(every, key=lambda o: (-(min(o[0], 4 - o[0]) + min(o[1], 4 - o[1])), o[2]))


def kernel(
    bg, value, height, obs_weight, index, counts, owner, table, out, load_recv,
    value_v, height_v, weight_v, index_v, counts_v, owner_v, table_v,
    message, received, fields, shared, load_send, rows_in, rows_out,
    small_sem, in_send, in_recv, out_send, out_recv, obs_send, obs_recv, load_sems,
):
    me = lax.axis_index("mem")
    tile = lax.axis_index("tile")
    z, x, core = me // 8, (me // 2) % 4, me % 2
    zs = [lax.rem(z + d, 4) * 8 for d in range(4)]
    xs = [lax.rem(x + d, 4) * 2 for d in range(4)]
    cores = [core, 1 - core]
    partners = [zs[dz] + (xs[dx] + cores[dc]) for dz, dx, dc in offsets()]
    tile_partners = [lax.rem(tile + d, N_TILE) for d in range(1, N_TILE)]
    small = [
        pltpu.make_async_copy(a, b, small_sem.at[i])
        for i, (a, b) in enumerate(
            zip(
                (value, height, obs_weight, index, counts, owner, table),
                (value_v, height_v, weight_v, index_v, counts_v, owner_v, table_v),
            )
        )
    ]
    for copy in small:
        copy.start()
    barrier = pltpu.get_barrier_semaphore()
    for p in partners:
        pl.semaphore_signal(barrier, inc=1, device_id=(p, tile), device_id_type=MESH)
    for q in tile_partners:
        pl.semaphore_signal(barrier, inc=1, device_id=(me, q), device_id_type=MESH)
    for copy in small:
        copy.wait()

    localised = jnp.zeros((OBS_L, COLS_T), F32)
    entry = index_v[...]
    table_row = table_v[...]
    for k in range(LOC_N):
        localised = jnp.where(entry == k, table_row[:, k : k + 1], localised)
    live = (me * OBS_L + iota((OBS_L, COLS_T), 0)) < counts_v[...]
    weights = jnp.where(live, localised * weight_v[...], 0.0)
    first = jnp.concatenate([value_v[...], height_v[...]], 0)
    second = jnp.concatenate([weights, jnp.zeros((OBS_L, COLS_T), F32)], 0)
    stack = []
    for b in range(4):
        stack += [first[:, 128 * b : 128 * b + 128], second[:, 128 * b : 128 * b + 128]]
    stack = swap_blocks(jnp.concatenate(stack, 0))
    column_load = jnp.sum(weights, 0, keepdims=True)
    right_half = jnp.concatenate([stack[16 * b + 8 : 16 * b + 16] for b in range(4)], 0)
    lane = iota((N_MEM, 128), 1)
    first_owner = iota((N_MEM, COLS_T), 0) * N_TILE
    owners = owner_v[...]
    for q in range(N_TILE):
        part = jnp.sum(
            jnp.where(first_owner + q == owners, column_load, 0.0), 1, keepdims=True
        )
        right_half = jnp.where(lane == 64 + q, part, right_half)
    left_half = jnp.concatenate([stack[16 * b : 16 * b + 8] for b in range(4)], 0)
    message[...] = jnp.concatenate([left_half, right_half], 1).reshape(N_MEM, 1, WIDTH)

    pl.semaphore_wait(barrier, N_MEM - 1 + N_TILE - 1)

    def send_rows(c):
        def source(p):
            return bg.at[pl.ds(pl.multiple_of(p * OWN + c * CHUNK, CHUNK), CHUNK)]

        for p in partners:
            pltpu.make_async_remote_copy(
                src_ref=source(p),
                dst_ref=rows_in.at[c, me],
                send_sem=in_send.at[c],
                recv_sem=in_recv.at[c],
                device_id=(p, tile),
                device_id_type=MESH,
            ).start()
        pltpu.make_async_copy(source(me), rows_in.at[c, me], in_recv.at[c]).start()

    for p in partners:
        pltpu.make_async_remote_copy(
            src_ref=message.at[p],
            dst_ref=received.at[me],
            send_sem=obs_send,
            recv_sem=obs_recv,
            device_id=(p, tile),
            device_id_type=MESH,
        ).start()
    pltpu.make_async_copy(message.at[me], received.at[me], obs_recv).start()
    for c in range(CHUNKS):
        send_rows(c)

    pltpu.make_async_copy(received, received, obs_recv).wait()
    arrived = received[...].reshape(N_MEM, WIDTH)
    arrived = jnp.concatenate([arrived, jnp.zeros((128 - N_MEM, WIDTH), F32)], 0).T
    for f in range(3):
        fields[f] = jnp.concatenate(
            [arrived[(4 * f + o) * OWN : (4 * f + o + 1) * OWN, :N_MEM] for o in range(OBS_L)], 1
        )
    loads = jnp.sum(arrived[192 : 192 + N_TILE], 1, keepdims=True)
    load_send[...] = jnp.broadcast_to(loads, (N_TILE, 128)).reshape(N_TILE, 1, 128)
    for q in tile_partners:
        pltpu.make_async_remote_copy(
            src_ref=load_send.at[q],
            dst_ref=load_recv.at[tile],
            send_sem=load_sems.at[0],
            recv_sem=load_sems.at[1],
            device_id=(me, q),
            device_id_type=MESH,
        ).start()
    pltpu.make_async_copy(load_send.at[tile], load_recv.at[tile], load_sems.at[1]).start()

    observe(fields, shared)

    def step(c, carry):
        pltpu.make_async_copy(rows_in.at[c], rows_in.at[c], in_recv.at[c]).wait()
        results = analyse(
            [rows_in[c, :, i, :] for i in range(CHUNK)],
            [
                [shared[c * (CHUNK // 2) + q, k] for k in range(3)]
                for q in range(CHUNK // 2)
            ],
        )
        for i in range(CHUNK):
            rows_out[c, :, i, :] = results[i]
        target = out.at[pl.ds(pl.multiple_of(me * OWN + c * CHUNK, CHUNK), CHUNK)]
        for p in partners:
            pltpu.make_async_remote_copy(
                src_ref=rows_out.at[c, p],
                dst_ref=target,
                send_sem=out_send.at[c],
                recv_sem=out_recv.at[c],
                device_id=(p, tile),
                device_id_type=MESH,
            ).start()
        pltpu.make_async_copy(rows_out.at[c, me], target, out_recv.at[c]).start()
        return carry

    lax.fori_loop(0, CHUNKS, step, 0)

    pltpu.make_async_copy(load_recv, load_recv, load_sems.at[1]).wait()
    sent = load_send.at[pl.ds(0, N_TILE - 1)]
    pltpu.make_async_copy(sent, sent, load_sems.at[0]).wait()
    sent = message.at[pl.ds(0, N_MEM - 1)]
    pltpu.make_async_copy(sent, sent, obs_send).wait()
    for c in range(CHUNKS):
        sent = rows_in.at[c, pl.ds(0, N_MEM - 1)]
        pltpu.make_async_copy(sent, sent, in_send.at[c]).wait()
        pltpu.make_async_copy(sent, sent, out_send.at[c]).wait()
        pltpu.make_async_copy(rows_out.at[c], rows_out.at[c], out_recv.at[c]).wait()


def finish(rows, parts, out, load_out, load_v, sems):
    rows_copy = pltpu.make_async_copy(rows, out, sems.at[0])
    rows_copy.start()
    load_v[...] = jnp.sum(parts[...], 0) * (1.0 / (OBS * CAP))
    load_copy = pltpu.make_async_copy(load_v, load_out, sems.at[1])
    load_copy.start()
    rows_copy.wait()
    load_copy.wait()


def per_device(background, obs_value, obs_height, obs_weight, counts, owner, loc_index, loc_table):
    hbm = pl.BlockSpec(memory_space=pl.ANY)

    def keep(x):
        return pltpu.with_memory_space_constraint(x, pltpu.HBM)

    dma = pltpu.SemaphoreType.DMA
    analysis, load = pl.pallas_call(
        kernel,
        out_shape=(
            jax.ShapeDtypeStruct((COLS_T, WIDTH), F32),
            jax.ShapeDtypeStruct((N_TILE, 1, 128), F32),
        ),
        in_specs=[hbm] * 8,
        out_specs=(hbm, hbm),
        scratch_shapes=[
            pltpu.VMEM((OBS_L, COLS_T), F32),
            pltpu.VMEM((OBS_L, COLS_T), F32),
            pltpu.VMEM((OBS_L, COLS_T), F32),
            pltpu.VMEM((OBS_L, COLS_T), jnp.int32),
            pltpu.VMEM((1, COLS_T), jnp.int32),
            pltpu.VMEM((1, COLS_T), jnp.int32),
            pltpu.VMEM((1, LOC_N), F32),
            pltpu.VMEM((N_MEM, 1, WIDTH), F32),
            pltpu.VMEM((N_MEM, 1, WIDTH), F32),
            pltpu.VMEM((3, OWN, OBS), F32),
            pltpu.VMEM((OWN // 2, 3, 64, 128), F32),
            pltpu.VMEM((N_TILE, 1, 128), F32),
            pltpu.VMEM((CHUNKS, N_MEM, CHUNK, WIDTH), F32),
            pltpu.VMEM((CHUNKS, N_MEM, CHUNK, WIDTH), F32),
            dma((7,)),
            dma((CHUNKS,)),
            dma((CHUNKS,)),
            dma((CHUNKS,)),
            dma((CHUNKS,)),
            dma,
            dma,
            dma((2,)),
        ],
        compiler_params=pltpu.CompilerParams(
            collective_id=0, has_side_effects=True, vmem_limit_bytes=16 << 20
        ),
    )(
        keep(background),
        keep(obs_value.T),
        keep(obs_height.T),
        keep(obs_weight.T),
        keep(loc_index.T),
        keep(counts.reshape(1, COLS_T)),
        keep(owner.reshape(1, COLS_T)),
        keep(loc_table.reshape(1, LOC_N)),
    )
    analysis, load = pl.pallas_call(
        finish,
        out_shape=(
            jax.ShapeDtypeStruct((COLS_T, WIDTH), F32),
            jax.ShapeDtypeStruct((1, 128), F32),
        ),
        in_specs=[hbm, pl.BlockSpec(memory_space=pltpu.VMEM)],
        out_specs=(hbm, hbm),
        scratch_shapes=[pltpu.VMEM((1, 128), F32), dma((2,))],
        compiler_params=pltpu.CompilerParams(vmem_limit_bytes=16 << 20),
    )(analysis, load)
    return analysis, load[0, :1]


def solution(mesh):
    placed = (
        P("tile", "mem"),
        P("tile", "mem"),
        P("tile", "mem"),
        P("tile", "mem"),
        P("tile"),
        P("tile", None),
        P("tile", "mem"),
        P(),
    )
    return jax.shard_map(
        per_device,
        mesh=mesh,
        in_specs=placed,
        out_specs=(P("tile", "mem"), P(("mem", "tile"))),
        check_vma=False,
    )
```

```python
import functools

import jax
import jax.numpy as jnp
from jax import lax
from jax.experimental import pallas as pl
from jax.experimental.pallas import tpu as pltpu
from jax.sharding import PartitionSpec as P

LEV = 64
OBS = 128
LOC_N = 16
CAP = 8
N_MEM = 32
N_TILE = 4
COLS_T = 512
OWN = COLS_T // N_MEM
CHUNK = 8
CHUNKS = OWN // CHUNK
OBS_L = OBS // N_MEM
WIDTH = 256
BY_START = [
    2 * chip + core
    for chip in sorted(range(N_MEM // 2), key=lambda k: 1.1 * (k // 4) + 0.45 * (k % 4))
    for core in (1, 0)
]

F32 = jnp.float32
BF16 = jnp.bfloat16
MESH = pl.DeviceIdType.MESH


def iota(shape, axis):
    return lax.broadcasted_iota(jnp.int32, shape, axis)


def split(x):
    high = x.astype(BF16)
    return high, (x - high.astype(F32)).astype(BF16)


def right_side(x, keep0, keep1):
    high, low = split(x)
    top = jnp.concatenate([high * keep0, low * keep0], 1)
    bottom = jnp.concatenate([high * keep1, low * keep1], 1)
    return jnp.concatenate([top, bottom, top, bottom], 0)


def product(a, right):
    high, low = split(a)
    both = jnp.dot(jnp.concatenate([high, low], 1), right, preferred_element_type=F32)
    return both[:, :128] + both[:, 128:]


def lane_masks():
    lane = iota((64, 128), 1)
    left = lane < 64
    keep0 = jnp.where(left, 1.0, 0.0).astype(BF16)
    keep1 = jnp.where(left, 0.0, 1.0).astype(BF16)
    return lane, iota((64, 128), 0), left, keep0, keep1


def observe(fields, shared):
    left = lane_masks()[2]
    level = iota((64, 128), 0).astype(F32)

    def pair(q, carry):
        both = []
        for j in (0, 1):
            value, height, weight = [fields[f, pl.ds(2 * q + j, 1), :] for f in range(3)]
            hat = jnp.maximum(0.0, 1.0 - jnp.abs(level - height))
            hat_next = jnp.maximum(0.0, 1.0 - jnp.abs((level + 1.0) - height))
            weighted = weight * hat
            terms = (weighted * hat, weighted * hat_next, weighted * value)
            both.append([jnp.sum(x, 1, keepdims=True) for x in terms])
        for k in range(3):
            shared[q, k] = jnp.where(left, both[0][k], both[1][k])
        return carry

    lax.fori_loop(0, OWN // 2, pair, 0)


def analyse(blocks, shared):
    lane, row, left, keep0, keep1 = lane_masks()
    left1 = left[:1]
    eye = jnp.where((lane & 63) == row, 1.0, 0.0)
    pairs = range(len(shared))

    def exchange(x, y):
        return jnp.where(left, x, pltpu.roll(y, 64, 1)), jnp.where(left, pltpu.roll(x, 64, 1), y)

    halves, centre, square, mean_col = [], [], [], []
    for q in pairs:
        x, y = [jnp.concatenate([b[:, :128], b[:, 128:]], 0) for b in blocks[2 * q : 2 * q + 2]]
        x = jnp.concatenate(exchange(x, y), 0)
        mean = jnp.sum(x, 0, keepdims=True) * (1.0 / 128.0)
        high, low = split(x - mean)
        both = lax.dot_general(
            jnp.concatenate([high, low], 0),
            jnp.concatenate([jnp.concatenate([high, low], 1)] * 2, 0),
            (((0,), (0,)), ((), ())),
            preferred_element_type=F32,
        )
        square.append(both[:, :128] + both[:, 128:])
        diagonal = eye * mean
        mean_col.append(
            jnp.where(
                left,
                jnp.sum(jnp.where(left, diagonal, 0.0), 1, keepdims=True),
                jnp.sum(jnp.where(left, 0.0, diagonal), 1, keepdims=True),
            )
        )
        halves.append(jnp.concatenate([high, low], 1))
        centre.append(mean)
    base, force = [], []
    for q in pairs:
        g = jnp.where(left, square[q][:64], square[q][64:])
        d, e, w = shared[q]

        def tridiagonal(m):
            return d * m + pltpu.roll(e * m, 1, 0) + e * pltpu.roll(m, 63, 0)

        w = w - tridiagonal(mean_col[q])
        base.append(tridiagonal(g))
        force.append(jnp.broadcast_to(jnp.sum(w * g, 0, keepdims=True), (16, 128)))
    right = [right_side(b, keep0, keep1) for b in base]
    out = [product(jnp.concatenate([base[q], force[q]], 0), right[q]) for q in pairs]
    cube = [product(out[q][:64], right[q]) for q in pairs]
    p, z, t, inverse = [], [], [], []
    for q in pairs:
        b, b2 = base[q], out[q][:64]
        trace = jnp.sum(eye * (254.0 * b + b2), 0, keepdims=True)
        norm2 = 127.0 * 127.0 * 128.0 + jnp.where(
            left1,
            jnp.sum(jnp.where(left1, trace, 0.0), 1, keepdims=True),
            jnp.sum(jnp.where(left1, 0.0, trace), 1, keepdims=True),
        )
        a = lax.rsqrt(norm2)
        u = 127.0 * a
        p.append(
            (u * (2.25 + u * (-1.5 + 0.25 * u))) * eye
            + (a * (2.25 + u * (-3.0 + 0.75 * u))) * b
            + (a * a * (-1.5 + 0.75 * u)) * b2
            + (a * a * a * 0.25) * cube[q]
        )
        z.append((1.5 - 0.5 * u) * eye - (0.5 * a) * b)
        t.append((1.5 - 0.5 * u) * force[q] - (0.5 * a) * out[q][64:])
        inverse.append(a)
    for sweep in range(3):
        right = [right_side(p[q], keep0, keep1) for q in pairs]
        out = [product(jnp.concatenate([p[q], z[q], t[q]], 0), right[q]) for q in pairs]
        cube = [product(out[q][:64], right[q]) for q in pairs]
        for q in pairs:
            z[q] = 1.5 * z[q] - 0.5 * out[q][64:128]
            t[q] = 1.5 * t[q] - 0.5 * out[q][128:]
            p[q] = 2.25 * p[q] - 1.5 * out[q][:64] + 0.25 * cube[q]
    results = []
    for q in pairs:
        out = product(jnp.concatenate([z[q], t[q]], 0), right_side(p[q], keep0, keep1))
        z[q] = 1.5 * z[q] - 0.5 * out[:64]
        t[q] = 1.5 * t[q] - 0.5 * out[64:]
    for q in pairs:
        t_halves = jnp.concatenate(split(t[q]), 1)
        both = jnp.dot(
            jnp.concatenate([halves[q], t_halves], 0),
            right_side(z[q], keep0, keep1),
            preferred_element_type=F32,
        )
        both = both[:, :128] + both[:, 128:]
        full = (centre[q] + inverse[q] * both[128:129]) + jnp.sqrt(127.0 * inverse[q]) * both[:128]
        for x in exchange(full[:64], full[64:]):
            results.append(jnp.concatenate([x[:32], x[32:]], 1))
    return results


def swap_blocks(x):
    row = iota(x.shape, 0)
    block = iota(x.shape, 1) // 16
    for s in (1, 2, 4):
        row_bit = (row // s) % 2
        block_bit = (block // s) % 2
        up = pltpu.roll(pltpu.roll(x, 64 - s, 0), 16 * s, 1)
        down = pltpu.roll(pltpu.roll(x, s, 0), 128 - 16 * s, 1)
        x = jnp.where(row_bit == block_bit, x, jnp.where(row_bit < block_bit, up, down))
    return x


def offsets():
    every = [(z, x, c) for z in range(4) for x in range(4) for c in range(2) if z or x or c]
    return sorted(every, key=lambda o: (-(min(o[0], 4 - o[0]) + min(o[1], 4 - o[1])), o[2]))


def kernel(
    bg, value, height, obs_weight, index, counts, owner, table, out, load_recv,
    value_v, height_v, weight_v, index_v, counts_v, owner_v, table_v,
    message, received, fields, shared, load_send, rows_in, rows_out,
    small_sem, in_send, in_recv, out_send, out_recv, obs_send, obs_recv, load_sems,
):
    me = lax.axis_index("mem")
    tile = lax.axis_index("tile")
    z, x, core = me // 8, (me // 2) % 4, me % 2
    zs = [lax.rem(z + d, 4) * 8 for d in range(4)]
    xs = [lax.rem(x + d, 4) * 2 for d in range(4)]
    cores = [core, 1 - core]
    partners = []
    for dz, dx, dc in offsets():
        chips = jnp.where(core == 0, zs[dz] + xs[dx], zs[-dx % 4] + xs[-dz % 4])
        partners.append(chips + cores[dc])
    tile_partners = [lax.rem(tile + d, N_TILE) for d in range(1, N_TILE)]
    small = [
        pltpu.make_async_copy(a, b, small_sem.at[i])
        for i, (a, b) in enumerate(
            zip(
                (value, height, obs_weight, index, counts, owner, table),
                (value_v, height_v, weight_v, index_v, counts_v, owner_v, table_v),
            )
        )
    ]
    for copy in small:
        copy.start()
    barrier = pltpu.get_barrier_semaphore()
    for p in partners:
        pl.semaphore_signal(barrier, inc=1, device_id=(p, tile), device_id_type=MESH)
    for q in tile_partners:
        pl.semaphore_signal(barrier, inc=1, device_id=(me, q), device_id_type=MESH)
    for copy in small:
        copy.wait()

    localised = jnp.zeros((OBS_L, COLS_T), F32)
    entry = index_v[...]
    table_row = table_v[...]
    for k in range(LOC_N):
        localised = jnp.where(entry == k, table_row[:, k : k + 1], localised)
    live = (me * OBS_L + iota((OBS_L, COLS_T), 0)) < counts_v[...]
    weights = jnp.where(live, localised * weight_v[...], 0.0)
    first = jnp.concatenate([value_v[...], height_v[...]], 0)
    second = jnp.concatenate([weights, jnp.zeros((OBS_L, COLS_T), F32)], 0)
    stack = []
    for b in range(4):
        stack += [first[:, 128 * b : 128 * b + 128], second[:, 128 * b : 128 * b + 128]]
    stack = swap_blocks(jnp.concatenate(stack, 0))
    column_load = jnp.sum(weights, 0, keepdims=True)
    right_half = jnp.concatenate([stack[16 * b + 8 : 16 * b + 16] for b in range(4)], 0)
    lane = iota((N_MEM, 128), 1)
    first_owner = iota((N_MEM, COLS_T), 0) * N_TILE
    owners = owner_v[...]
    for q in range(N_TILE):
        part = jnp.sum(
            jnp.where(first_owner + q == owners, column_load, 0.0), 1, keepdims=True
        )
        right_half = jnp.where(lane == 64 + q, part, right_half)
    left_half = jnp.concatenate([stack[16 * b : 16 * b + 8] for b in range(4)], 0)
    message[...] = jnp.concatenate([left_half, right_half], 1).reshape(N_MEM, 1, WIDTH)

    pl.semaphore_wait(barrier, N_MEM - 1 + N_TILE - 1)

    def send_rows(c):
        def source(p):
            return bg.at[pl.ds(pl.multiple_of(p * OWN + c * CHUNK, CHUNK), CHUNK)]

        for p in partners:
            pltpu.make_async_remote_copy(
                src_ref=source(p),
                dst_ref=rows_in.at[c, me],
                send_sem=in_send.at[c],
                recv_sem=in_recv.at[c],
                device_id=(p, tile),
                device_id_type=MESH,
            ).start()
        pltpu.make_async_copy(source(me), rows_in.at[c, me], in_recv.at[c]).start()

    for p in partners:
        pltpu.make_async_remote_copy(
            src_ref=message.at[p],
            dst_ref=received.at[me],
            send_sem=obs_send,
            recv_sem=obs_recv,
            device_id=(p, tile),
            device_id_type=MESH,
        ).start()
    pltpu.make_async_copy(message.at[me], received.at[me], obs_recv).start()
    for c in range(CHUNKS):
        send_rows(c)

    pltpu.make_async_copy(received, received, obs_recv).wait()
    arrived = received[...].reshape(N_MEM, WIDTH)
    arrived = jnp.concatenate([arrived, jnp.zeros((128 - N_MEM, WIDTH), F32)], 0).T
    for f in range(3):
        fields[f] = jnp.concatenate(
            [arrived[(4 * f + o) * OWN : (4 * f + o + 1) * OWN, :N_MEM] for o in range(OBS_L)], 1
        )
    loads = jnp.sum(arrived[192 : 192 + N_TILE], 1, keepdims=True)
    load_send[...] = jnp.broadcast_to(loads, (N_TILE, 128)).reshape(N_TILE, 1, 128)
    for q in tile_partners:
        pltpu.make_async_remote_copy(
            src_ref=load_send.at[q],
            dst_ref=load_recv.at[tile],
            send_sem=load_sems.at[0],
            recv_sem=load_sems.at[1],
            device_id=(me, q),
            device_id_type=MESH,
        ).start()
    pltpu.make_async_copy(load_send.at[tile], load_recv.at[tile], load_sems.at[1]).start()

    observe(fields, shared)

    def step(c, carry):
        pltpu.make_async_copy(rows_in.at[c], rows_in.at[c], in_recv.at[c]).wait()
        results = analyse(
            [rows_in[c, :, i, :] for i in range(CHUNK)],
            [
                [shared[c * (CHUNK // 2) + q, k] for k in range(3)]
                for q in range(CHUNK // 2)
            ],
        )
        for i in range(CHUNK):
            rows_out[c, :, i, :] = results[i]
        target = out.at[pl.ds(pl.multiple_of(me * OWN + c * CHUNK, CHUNK), CHUNK)]

        def send_out(p):
            pltpu.make_async_remote_copy(
                src_ref=rows_out.at[c, p],
                dst_ref=target,
                send_sem=out_send.at[c],
                recv_sem=out_recv.at[c],
                device_id=(p, tile),
                device_id_type=MESH,
            ).start()

        for p in BY_START:
            pl.when(p != me)(functools.partial(send_out, p))
        pltpu.make_async_copy(rows_out.at[c, me], target, out_recv.at[c]).start()
        return carry

    lax.fori_loop(0, CHUNKS, step, 0)

    pltpu.make_async_copy(load_recv, load_recv, load_sems.at[1]).wait()
    sent = load_send.at[pl.ds(0, N_TILE - 1)]
    pltpu.make_async_copy(sent, sent, load_sems.at[0]).wait()
    sent = message.at[pl.ds(0, N_MEM - 1)]
    pltpu.make_async_copy(sent, sent, obs_send).wait()
    for c in range(CHUNKS):
        sent = rows_in.at[c, pl.ds(0, N_MEM - 1)]
        pltpu.make_async_copy(sent, sent, in_send.at[c]).wait()
        pltpu.make_async_copy(sent, sent, out_send.at[c]).wait()
        pltpu.make_async_copy(rows_out.at[c], rows_out.at[c], out_recv.at[c]).wait()


def finish(rows, parts, out, load_out, load_v, sems):
    rows_copy = pltpu.make_async_copy(rows, out, sems.at[0])
    rows_copy.start()
    load_v[...] = jnp.sum(parts[...], 0) * (1.0 / (OBS * CAP))
    load_copy = pltpu.make_async_copy(load_v, load_out, sems.at[1])
    load_copy.start()
    rows_copy.wait()
    load_copy.wait()


def per_device(background, obs_value, obs_height, obs_weight, counts, owner, loc_index, loc_table):
    hbm = pl.BlockSpec(memory_space=pl.ANY)

    def keep(x):
        return pltpu.with_memory_space_constraint(x, pltpu.HBM)

    dma = pltpu.SemaphoreType.DMA
    analysis, load = pl.pallas_call(
        kernel,
        out_shape=(
            jax.ShapeDtypeStruct((COLS_T, WIDTH), F32),
            jax.ShapeDtypeStruct((N_TILE, 1, 128), F32),
        ),
        in_specs=[hbm] * 8,
        out_specs=(hbm, hbm),
        scratch_shapes=[
            pltpu.VMEM((OBS_L, COLS_T), F32),
            pltpu.VMEM((OBS_L, COLS_T), F32),
            pltpu.VMEM((OBS_L, COLS_T), F32),
            pltpu.VMEM((OBS_L, COLS_T), jnp.int32),
            pltpu.VMEM((1, COLS_T), jnp.int32),
            pltpu.VMEM((1, COLS_T), jnp.int32),
            pltpu.VMEM((1, LOC_N), F32),
            pltpu.VMEM((N_MEM, 1, WIDTH), F32),
            pltpu.VMEM((N_MEM, 1, WIDTH), F32),
            pltpu.VMEM((3, OWN, OBS), F32),
            pltpu.VMEM((OWN // 2, 3, 64, 128), F32),
            pltpu.VMEM((N_TILE, 1, 128), F32),
            pltpu.VMEM((CHUNKS, N_MEM, CHUNK, WIDTH), F32),
            pltpu.VMEM((CHUNKS, N_MEM, CHUNK, WIDTH), F32),
            dma((7,)),
            dma((CHUNKS,)),
            dma((CHUNKS,)),
            dma((CHUNKS,)),
            dma((CHUNKS,)),
            dma,
            dma,
            dma((2,)),
        ],
        compiler_params=pltpu.CompilerParams(
            collective_id=0, has_side_effects=True, vmem_limit_bytes=16 << 20
        ),
    )(
        keep(background),
        keep(obs_value.T),
        keep(obs_height.T),
        keep(obs_weight.T),
        keep(loc_index.T),
        keep(counts.reshape(1, COLS_T)),
        keep(owner.reshape(1, COLS_T)),
        keep(loc_table.reshape(1, LOC_N)),
    )
    analysis, load = pl.pallas_call(
        finish,
        out_shape=(
            jax.ShapeDtypeStruct((COLS_T, WIDTH), F32),
            jax.ShapeDtypeStruct((1, 128), F32),
        ),
        in_specs=[hbm, pl.BlockSpec(memory_space=pltpu.VMEM)],
        out_specs=(hbm, hbm),
        scratch_shapes=[pltpu.VMEM((1, 128), F32), dma((2,))],
        compiler_params=pltpu.CompilerParams(vmem_limit_bytes=16 << 20),
    )(analysis, load)
    return analysis, load[0, :1]


def solution(mesh):
    placed = (
        P("tile", "mem"),
        P("tile", "mem"),
        P("tile", "mem"),
        P("tile", "mem"),
        P("tile"),
        P("tile", None),
        P("tile", "mem"),
        P(),
    )
    return jax.shard_map(
        per_device,
        mesh=mesh,
        in_specs=placed,
        out_specs=(P("tile", "mem"), P(("mem", "tile"))),
        check_vma=False,
    )
```

```python
import functools

import jax
import jax.numpy as jnp
from jax import lax
from jax.experimental import pallas as pl
from jax.experimental.pallas import tpu as pltpu
from jax.sharding import PartitionSpec as P

LEV = 64
OBS = 128
LOC_N = 16
CAP = 8
N_MEM = 32
N_TILE = 4
COLS_T = 512
OWN = COLS_T // N_MEM
CHUNK = 8
CHUNKS = OWN // CHUNK
OBS_L = OBS // N_MEM
WIDTH = 256
BY_START = [
    2 * chip + core
    for chip in sorted(range(N_MEM // 2), key=lambda k: 1.1 * (k // 4) + 0.45 * (k % 4))
    for core in (1, 0)
]

F32 = jnp.float32
BF16 = jnp.bfloat16
MESH = pl.DeviceIdType.MESH


def iota(shape, axis):
    return lax.broadcasted_iota(jnp.int32, shape, axis)


def split(x):
    high = x.astype(BF16)
    return high, (x - high.astype(F32)).astype(BF16)


def right_side(x, keep0, keep1):
    high, low = split(x)
    top = jnp.concatenate([high * keep0, low * keep0], 1)
    bottom = jnp.concatenate([high * keep1, low * keep1], 1)
    return jnp.concatenate([top, bottom, top, bottom], 0)


def product(a, right):
    high, low = split(a)
    both = jnp.dot(jnp.concatenate([high, low], 1), right, preferred_element_type=F32)
    return both[:, :128] + both[:, 128:]


def lane_masks():
    lane = iota((64, 128), 1)
    left = lane < 64
    keep0 = jnp.where(left, 1.0, 0.0).astype(BF16)
    keep1 = jnp.where(left, 0.0, 1.0).astype(BF16)
    return lane, iota((64, 128), 0), left, keep0, keep1


def observe(fields, shared):
    left = lane_masks()[2]
    level = iota((64, 128), 0).astype(F32)

    def pair(q, carry):
        both = []
        for j in (0, 1):
            value, height, weight = [fields[f, pl.ds(2 * q + j, 1), :] for f in range(3)]
            hat = jnp.maximum(0.0, 1.0 - jnp.abs(level - height))
            hat_next = jnp.maximum(0.0, 1.0 - jnp.abs((level + 1.0) - height))
            weighted = weight * hat
            terms = (weighted * hat, weighted * hat_next, weighted * value)
            both.append([jnp.sum(x, 1, keepdims=True) for x in terms])
        for k in range(3):
            shared[q, k] = jnp.where(left, both[0][k], both[1][k])
        return carry

    lax.fori_loop(0, OWN // 2, pair, 0)


def analyse(blocks, shared):
    lane, row, left, keep0, keep1 = lane_masks()
    left1 = left[:1]
    eye = jnp.where((lane & 63) == row, 1.0, 0.0)
    pairs = range(len(shared))

    def exchange(x, y):
        return jnp.where(left, x, pltpu.roll(y, 64, 1)), jnp.where(left, pltpu.roll(x, 64, 1), y)

    halves, centre, square, mean_col = [], [], [], []
    for q in pairs:
        x, y = [jnp.concatenate([b[:, :128], b[:, 128:]], 0) for b in blocks[2 * q : 2 * q + 2]]
        x = jnp.concatenate(exchange(x, y), 0)
        mean = jnp.sum(x, 0, keepdims=True) * (1.0 / 128.0)
        high, low = split(x - mean)
        both = lax.dot_general(
            jnp.concatenate([high, low], 0),
            jnp.concatenate([jnp.concatenate([high, low], 1)] * 2, 0),
            (((0,), (0,)), ((), ())),
            preferred_element_type=F32,
        )
        square.append(both[:, :128] + both[:, 128:])
        diagonal = eye * mean
        mean_col.append(
            jnp.where(
                left,
                jnp.sum(jnp.where(left, diagonal, 0.0), 1, keepdims=True),
                jnp.sum(jnp.where(left, 0.0, diagonal), 1, keepdims=True),
            )
        )
        halves.append(jnp.concatenate([high, low], 1))
        centre.append(mean)
    base, force = [], []
    for q in pairs:
        g = jnp.where(left, square[q][:64], square[q][64:])
        d, e, w = shared[q]

        def tridiagonal(m):
            return d * m + pltpu.roll(e * m, 1, 0) + e * pltpu.roll(m, 63, 0)

        w = w - tridiagonal(mean_col[q])
        base.append(tridiagonal(g))
        force.append(jnp.broadcast_to(jnp.sum(w * g, 0, keepdims=True), (16, 128)))
    right = [right_side(b, keep0, keep1) for b in base]
    out = [product(jnp.concatenate([base[q], force[q]], 0), right[q]) for q in pairs]
    cube = [product(out[q][:64], right[q]) for q in pairs]
    p, z, t, inverse = [], [], [], []
    for q in pairs:
        b, b2 = base[q], out[q][:64]
        trace = jnp.sum(eye * (254.0 * b + b2), 0, keepdims=True)
        norm2 = 127.0 * 127.0 * 128.0 + jnp.where(
            left1,
            jnp.sum(jnp.where(left1, trace, 0.0), 1, keepdims=True),
            jnp.sum(jnp.where(left1, 0.0, trace), 1, keepdims=True),
        )
        a = lax.rsqrt(norm2)
        u = 127.0 * a
        p.append(
            (u * (2.25 + u * (-1.5 + 0.25 * u))) * eye
            + (a * (2.25 + u * (-3.0 + 0.75 * u))) * b
            + (a * a * (-1.5 + 0.75 * u)) * b2
            + (a * a * a * 0.25) * cube[q]
        )
        z.append((1.5 - 0.5 * u) * eye - (0.5 * a) * b)
        t.append((1.5 - 0.5 * u) * force[q] - (0.5 * a) * out[q][64:])
        inverse.append(a)
    for sweep in range(3):
        right = [right_side(p[q], keep0, keep1) for q in pairs]
        out = [product(jnp.concatenate([p[q], z[q], t[q]], 0), right[q]) for q in pairs]
        cube = [product(out[q][:64], right[q]) for q in pairs]
        for q in pairs:
            z[q] = 1.5 * z[q] - 0.5 * out[q][64:128]
            t[q] = 1.5 * t[q] - 0.5 * out[q][128:]
            p[q] = 2.25 * p[q] - 1.5 * out[q][:64] + 0.25 * cube[q]
    results = []
    for q in pairs:
        out = product(jnp.concatenate([z[q], t[q]], 0), right_side(p[q], keep0, keep1))
        z[q] = 1.5 * z[q] - 0.5 * out[:64]
        t[q] = 1.5 * t[q] - 0.5 * out[64:]
    for q in pairs:
        t_halves = jnp.concatenate(split(t[q]), 1)
        both = jnp.dot(
            jnp.concatenate([halves[q], t_halves], 0),
            right_side(z[q], keep0, keep1),
            preferred_element_type=F32,
        )
        both = both[:, :128] + both[:, 128:]
        full = (centre[q] + inverse[q] * both[128:129]) + jnp.sqrt(127.0 * inverse[q]) * both[:128]
        for x in exchange(full[:64], full[64:]):
            results.append(jnp.concatenate([x[:32], x[32:]], 1))
    return results


def swap_blocks(x):
    row = iota(x.shape, 0)
    block = iota(x.shape, 1) // 16
    for s in (1, 2, 4):
        row_bit = (row // s) % 2
        block_bit = (block // s) % 2
        up = pltpu.roll(pltpu.roll(x, 64 - s, 0), 16 * s, 1)
        down = pltpu.roll(pltpu.roll(x, s, 0), 128 - 16 * s, 1)
        x = jnp.where(row_bit == block_bit, x, jnp.where(row_bit < block_bit, up, down))
    return x


def offsets():
    every = [(z, x, c) for z in range(4) for x in range(4) for c in range(2) if z or x or c]
    return sorted(every, key=lambda o: (-(min(o[0], 4 - o[0]) + min(o[1], 4 - o[1])), o[2]))


def kernel(
    bg, value, height, obs_weight, index, counts, owner, table, out, load_recv,
    value_v, height_v, weight_v, index_v, counts_v, owner_v, table_v,
    message, received, fields, shared, load_send, rows_in, rows_out,
    tile_ready, small_sem, in_send, in_recv, out_send, out_recv, obs_send, obs_recv, load_sems,
):
    me = lax.axis_index("mem")
    tile = lax.axis_index("tile")
    z, x, core = me // 8, (me // 2) % 4, me % 2
    zs = [lax.rem(z + d, 4) * 8 for d in range(4)]
    xs = [lax.rem(x + d, 4) * 2 for d in range(4)]
    cores = [core, 1 - core]
    partners = []
    for dz, dx, dc in offsets():
        chips = jnp.where(core == 0, zs[dz] + xs[dx], zs[-dx % 4] + xs[-dz % 4])
        partners.append(chips + cores[dc])
    tile_partners = [lax.rem(tile + d, N_TILE) for d in range(1, N_TILE)]
    small = [
        pltpu.make_async_copy(a, b, small_sem.at[i])
        for i, (a, b) in enumerate(
            zip(
                (value, height, obs_weight, index, counts, owner, table),
                (value_v, height_v, weight_v, index_v, counts_v, owner_v, table_v),
            )
        )
    ]
    for copy in small:
        copy.start()
    barrier = pltpu.get_barrier_semaphore()
    for p in partners:
        pl.semaphore_signal(barrier, inc=1, device_id=(p, tile), device_id_type=MESH)

    def greet(there, semaphore, q):
        @pl.when(there)
        def _():
            pl.semaphore_signal(semaphore, inc=1, device_id=(me, q), device_id_type=MESH)

    for q in tile_partners:
        greet(q > tile, barrier, q)
    for copy in small:
        copy.wait()

    localised = jnp.zeros((OBS_L, COLS_T), F32)
    entry = index_v[...]
    table_row = table_v[...]
    for k in range(LOC_N):
        localised = jnp.where(entry == k, table_row[:, k : k + 1], localised)
    live = (me * OBS_L + iota((OBS_L, COLS_T), 0)) < counts_v[...]
    weights = jnp.where(live, localised * weight_v[...], 0.0)
    first = jnp.concatenate([value_v[...], height_v[...]], 0)
    second = jnp.concatenate([weights, jnp.zeros((OBS_L, COLS_T), F32)], 0)
    stack = []
    for b in range(4):
        stack += [first[:, 128 * b : 128 * b + 128], second[:, 128 * b : 128 * b + 128]]
    stack = swap_blocks(jnp.concatenate(stack, 0))
    column_load = jnp.sum(weights, 0, keepdims=True)
    right_half = jnp.concatenate([stack[16 * b + 8 : 16 * b + 16] for b in range(4)], 0)
    lane = iota((N_MEM, 128), 1)
    first_owner = iota((N_MEM, COLS_T), 0) * N_TILE
    owners = owner_v[...]
    for q in range(N_TILE):
        part = jnp.sum(
            jnp.where(first_owner + q == owners, column_load, 0.0), 1, keepdims=True
        )
        right_half = jnp.where(lane == 64 + q, part, right_half)
    left_half = jnp.concatenate([stack[16 * b : 16 * b + 8] for b in range(4)], 0)
    message[...] = jnp.concatenate([left_half, right_half], 1).reshape(N_MEM, 1, WIDTH)

    pl.semaphore_wait(barrier, N_MEM - 1 + tile)

    def send_rows(c):
        def source(p):
            return bg.at[pl.ds(pl.multiple_of(p * OWN + c * CHUNK, CHUNK), CHUNK)]

        for p in partners:
            pltpu.make_async_remote_copy(
                src_ref=source(p),
                dst_ref=rows_in.at[c, me],
                send_sem=in_send.at[c],
                recv_sem=in_recv.at[c],
                device_id=(p, tile),
                device_id_type=MESH,
            ).start()
        pltpu.make_async_copy(source(me), rows_in.at[c, me], in_recv.at[c]).start()

    for p in partners:
        pltpu.make_async_remote_copy(
            src_ref=message.at[p],
            dst_ref=received.at[me],
            send_sem=obs_send,
            recv_sem=obs_recv,
            device_id=(p, tile),
            device_id_type=MESH,
        ).start()
    pltpu.make_async_copy(message.at[me], received.at[me], obs_recv).start()
    for c in range(CHUNKS):
        send_rows(c)

    for q in tile_partners:
        greet(q < tile, tile_ready, q)
    pltpu.make_async_copy(received, received, obs_recv).wait()
    arrived = received[...].reshape(N_MEM, WIDTH)
    arrived = jnp.concatenate([arrived, jnp.zeros((128 - N_MEM, WIDTH), F32)], 0).T
    for f in range(3):
        fields[f] = jnp.concatenate(
            [arrived[(4 * f + o) * OWN : (4 * f + o + 1) * OWN, :N_MEM] for o in range(OBS_L)], 1
        )
    loads = jnp.sum(arrived[192 : 192 + N_TILE], 1, keepdims=True)
    load_send[...] = jnp.broadcast_to(loads, (N_TILE, 128)).reshape(N_TILE, 1, 128)

    @pl.when(tile < N_TILE - 1)
    def _():
        pl.semaphore_wait(tile_ready, N_TILE - 1 - tile)

    for q in tile_partners:
        pltpu.make_async_remote_copy(
            src_ref=load_send.at[q],
            dst_ref=load_recv.at[tile],
            send_sem=load_sems.at[0],
            recv_sem=load_sems.at[1],
            device_id=(me, q),
            device_id_type=MESH,
        ).start()
    pltpu.make_async_copy(load_send.at[tile], load_recv.at[tile], load_sems.at[1]).start()

    observe(fields, shared)

    def step(c, carry):
        pltpu.make_async_copy(rows_in.at[c], rows_in.at[c], in_recv.at[c]).wait()
        results = analyse(
            [rows_in[c, :, i, :] for i in range(CHUNK)],
            [
                [shared[c * (CHUNK // 2) + q, k] for k in range(3)]
                for q in range(CHUNK // 2)
            ],
        )
        for i in range(CHUNK):
            rows_out[c, :, i, :] = results[i]
        target = out.at[pl.ds(pl.multiple_of(me * OWN + c * CHUNK, CHUNK), CHUNK)]

        def send_out(p):
            pltpu.make_async_remote_copy(
                src_ref=rows_out.at[c, p],
                dst_ref=target,
                send_sem=out_send.at[c],
                recv_sem=out_recv.at[c],
                device_id=(p, tile),
                device_id_type=MESH,
            ).start()

        for p in BY_START:
            pl.when(p != me)(functools.partial(send_out, p))
        pltpu.make_async_copy(rows_out.at[c, me], target, out_recv.at[c]).start()
        return carry

    lax.fori_loop(0, CHUNKS, step, 0)

    pltpu.make_async_copy(load_recv, load_recv, load_sems.at[1]).wait()
    sent = load_send.at[pl.ds(0, N_TILE - 1)]
    pltpu.make_async_copy(sent, sent, load_sems.at[0]).wait()
    sent = message.at[pl.ds(0, N_MEM - 1)]
    pltpu.make_async_copy(sent, sent, obs_send).wait()
    for c in range(CHUNKS):
        sent = rows_in.at[c, pl.ds(0, N_MEM - 1)]
        pltpu.make_async_copy(sent, sent, in_send.at[c]).wait()
        pltpu.make_async_copy(sent, sent, out_send.at[c]).wait()
        pltpu.make_async_copy(rows_out.at[c], rows_out.at[c], out_recv.at[c]).wait()


def finish(rows, parts, out, load_out, load_v, sems):
    rows_copy = pltpu.make_async_copy(rows, out, sems.at[0])
    rows_copy.start()
    load_v[...] = jnp.sum(parts[...], 0) * (1.0 / (OBS * CAP))
    load_copy = pltpu.make_async_copy(load_v, load_out, sems.at[1])
    load_copy.start()
    rows_copy.wait()
    load_copy.wait()


def per_device(background, obs_value, obs_height, obs_weight, counts, owner, loc_index, loc_table):
    hbm = pl.BlockSpec(memory_space=pl.ANY)

    def keep(x):
        return pltpu.with_memory_space_constraint(x, pltpu.HBM)

    dma = pltpu.SemaphoreType.DMA
    analysis, load = pl.pallas_call(
        kernel,
        out_shape=(
            jax.ShapeDtypeStruct((COLS_T, WIDTH), F32),
            jax.ShapeDtypeStruct((N_TILE, 1, 128), F32),
        ),
        in_specs=[hbm] * 8,
        out_specs=(hbm, hbm),
        scratch_shapes=[
            pltpu.VMEM((OBS_L, COLS_T), F32),
            pltpu.VMEM((OBS_L, COLS_T), F32),
            pltpu.VMEM((OBS_L, COLS_T), F32),
            pltpu.VMEM((OBS_L, COLS_T), jnp.int32),
            pltpu.VMEM((1, COLS_T), jnp.int32),
            pltpu.VMEM((1, COLS_T), jnp.int32),
            pltpu.VMEM((1, LOC_N), F32),
            pltpu.VMEM((N_MEM, 1, WIDTH), F32),
            pltpu.VMEM((N_MEM, 1, WIDTH), F32),
            pltpu.VMEM((3, OWN, OBS), F32),
            pltpu.VMEM((OWN // 2, 3, 64, 128), F32),
            pltpu.VMEM((N_TILE, 1, 128), F32),
            pltpu.VMEM((CHUNKS, N_MEM, CHUNK, WIDTH), F32),
            pltpu.VMEM((CHUNKS, N_MEM, CHUNK, WIDTH), F32),
            pltpu.SemaphoreType.REGULAR,
            dma((7,)),
            dma((CHUNKS,)),
            dma((CHUNKS,)),
            dma((CHUNKS,)),
            dma((CHUNKS,)),
            dma,
            dma,
            dma((2,)),
        ],
        compiler_params=pltpu.CompilerParams(
            collective_id=0, has_side_effects=True, vmem_limit_bytes=16 << 20
        ),
    )(
        keep(background),
        keep(obs_value.T),
        keep(obs_height.T),
        keep(obs_weight.T),
        keep(loc_index.T),
        keep(counts.reshape(1, COLS_T)),
        keep(owner.reshape(1, COLS_T)),
        keep(loc_table.reshape(1, LOC_N)),
    )
    analysis, load = pl.pallas_call(
        finish,
        out_shape=(
            jax.ShapeDtypeStruct((COLS_T, WIDTH), F32),
            jax.ShapeDtypeStruct((1, 128), F32),
        ),
        in_specs=[hbm, pl.BlockSpec(memory_space=pltpu.VMEM)],
        out_specs=(hbm, hbm),
        scratch_shapes=[pltpu.VMEM((1, 128), F32), dma((2,))],
        compiler_params=pltpu.CompilerParams(vmem_limit_bytes=16 << 20),
    )(analysis, load)
    return analysis, load[0, :1]


def solution(mesh):
    placed = (
        P("tile", "mem"),
        P("tile", "mem"),
        P("tile", "mem"),
        P("tile", "mem"),
        P("tile"),
        P("tile", None),
        P("tile", "mem"),
        P(),
    )
    return jax.shard_map(
        per_device,
        mesh=mesh,
        in_specs=placed,
        out_specs=(P("tile", "mem"), P(("mem", "tile"))),
        check_vma=False,
    )
```

```python
import functools

import jax
import jax.numpy as jnp
from jax import lax
from jax.experimental import pallas as pl
from jax.experimental.pallas import tpu as pltpu
from jax.sharding import PartitionSpec as P

LEV = 64
OBS = 128
LOC_N = 16
CAP = 8
N_MEM = 32
N_TILE = 4
COLS_T = 512
OWN = COLS_T // N_MEM
CHUNK = 8
CHUNKS = OWN // CHUNK
OBS_L = OBS // N_MEM
WIDTH = 256
BY_START = [
    2 * chip + core
    for chip in sorted(range(N_MEM // 2), key=lambda k: 1.1 * (k // 4) + 0.45 * (k % 4))
    for core in (1, 0)
]

F32 = jnp.float32
BF16 = jnp.bfloat16
MESH = pl.DeviceIdType.MESH


def iota(shape, axis):
    return lax.broadcasted_iota(jnp.int32, shape, axis)


def split(x):
    high = x.astype(BF16)
    return high, (x - high.astype(F32)).astype(BF16)


def right_side(x, keep0, keep1):
    high, low = split(x)
    top = jnp.concatenate([high * keep0, low * keep0], 1)
    bottom = jnp.concatenate([high * keep1, low * keep1], 1)
    return jnp.concatenate([top, bottom, top, bottom], 0)


def product(a, right):
    high, low = split(a)
    both = jnp.dot(jnp.concatenate([high, low], 1), right, preferred_element_type=F32)
    return both[:, :128] + both[:, 128:]


def lane_masks():
    lane = iota((64, 128), 1)
    left = lane < 64
    keep0 = jnp.where(left, 1.0, 0.0).astype(BF16)
    keep1 = jnp.where(left, 0.0, 1.0).astype(BF16)
    return lane, iota((64, 128), 0), left, keep0, keep1


def observe(fields, shared):
    left = lane_masks()[2]
    level = iota((64, 128), 0).astype(F32)

    def pair(q, carry):
        both = []
        for j in (0, 1):
            value, height, weight = [fields[f, pl.ds(2 * q + j, 1), :] for f in range(3)]
            hat = jnp.maximum(0.0, 1.0 - jnp.abs(level - height))
            hat_next = jnp.maximum(0.0, 1.0 - jnp.abs((level + 1.0) - height))
            weighted = weight * hat
            terms = (weighted * hat, weighted * hat_next, weighted * value)
            both.append([jnp.sum(x, 1, keepdims=True) for x in terms])
        for k in range(3):
            shared[q, k] = jnp.where(left, both[0][k], both[1][k])
        return carry

    lax.fori_loop(0, OWN // 2, pair, 0)


def analyse(blocks, shared):
    lane, row, left, keep0, keep1 = lane_masks()
    left1 = left[:1]
    eye = jnp.where((lane & 63) == row, 1.0, 0.0)
    pairs = range(len(shared))

    def exchange(x, y):
        return jnp.where(left, x, pltpu.roll(y, 64, 1)), jnp.where(left, pltpu.roll(x, 64, 1), y)

    halves, centre, square, mean_col = [], [], [], []
    for q in pairs:
        x, y = [jnp.concatenate([b[:, :128], b[:, 128:]], 0) for b in blocks[2 * q : 2 * q + 2]]
        x = jnp.concatenate(exchange(x, y), 0)
        mean = jnp.sum(x, 0, keepdims=True) * (1.0 / 128.0)
        high, low = split(x - mean)
        both = lax.dot_general(
            jnp.concatenate([high, low], 0),
            jnp.concatenate([jnp.concatenate([high, low], 1)] * 2, 0),
            (((0,), (0,)), ((), ())),
            preferred_element_type=F32,
        )
        square.append(both[:, :128] + both[:, 128:])
        diagonal = eye * mean
        mean_col.append(
            jnp.where(
                left,
                jnp.sum(jnp.where(left, diagonal, 0.0), 1, keepdims=True),
                jnp.sum(jnp.where(left, 0.0, diagonal), 1, keepdims=True),
            )
        )
        halves.append(jnp.concatenate([high, low], 1))
        centre.append(mean)
    base, force = [], []
    for q in pairs:
        g = jnp.where(left, square[q][:64], square[q][64:])
        d, e, w = shared[q]

        def tridiagonal(m):
            return d * m + pltpu.roll(e * m, 1, 0) + e * pltpu.roll(m, 63, 0)

        w = w - tridiagonal(mean_col[q])
        base.append(tridiagonal(g))
        force.append(jnp.broadcast_to(jnp.sum(w * g, 0, keepdims=True), (16, 128)))
    right = [right_side(b, keep0, keep1) for b in base]
    out = [product(jnp.concatenate([base[q], force[q]], 0), right[q]) for q in pairs]
    cube = [product(out[q][:64], right[q]) for q in pairs]
    p, z, t, inverse = [], [], [], []
    for q in pairs:
        b, b2 = base[q], out[q][:64]
        trace = jnp.sum(eye * (254.0 * b + b2), 0, keepdims=True)
        norm2 = 127.0 * 127.0 * 128.0 + jnp.where(
            left1,
            jnp.sum(jnp.where(left1, trace, 0.0), 1, keepdims=True),
            jnp.sum(jnp.where(left1, 0.0, trace), 1, keepdims=True),
        )
        a = lax.rsqrt(norm2)
        u = 127.0 * a
        p.append(
            (u * (2.25 + u * (-1.5 + 0.25 * u))) * eye
            + (a * (2.25 + u * (-3.0 + 0.75 * u))) * b
            + (a * a * (-1.5 + 0.75 * u)) * b2
            + (a * a * a * 0.25) * cube[q]
        )
        z.append((1.5 - 0.5 * u) * eye - (0.5 * a) * b)
        t.append((1.5 - 0.5 * u) * force[q] - (0.5 * a) * out[q][64:])
        inverse.append(a)
    for sweep in range(3):
        right = [right_side(p[q], keep0, keep1) for q in pairs]
        out = [product(jnp.concatenate([p[q], z[q], t[q]], 0), right[q]) for q in pairs]
        cube = [product(out[q][:64], right[q]) for q in pairs]
        for q in pairs:
            z[q] = 1.5 * z[q] - 0.5 * out[q][64:128]
            t[q] = 1.5 * t[q] - 0.5 * out[q][128:]
            p[q] = 2.25 * p[q] - 1.5 * out[q][:64] + 0.25 * cube[q]
    results = []
    for q in pairs:
        out = product(jnp.concatenate([z[q], t[q]], 0), right_side(p[q], keep0, keep1))
        z[q] = 1.5 * z[q] - 0.5 * out[:64]
        t[q] = 1.5 * t[q] - 0.5 * out[64:]
    for q in pairs:
        t_halves = jnp.concatenate(split(t[q]), 1)
        both = jnp.dot(
            jnp.concatenate([halves[q], t_halves], 0),
            right_side(z[q], keep0, keep1),
            preferred_element_type=F32,
        )
        both = both[:, :128] + both[:, 128:]
        full = (centre[q] + inverse[q] * both[128:129]) + jnp.sqrt(127.0 * inverse[q]) * both[:128]
        for x in exchange(full[:64], full[64:]):
            results.append(jnp.concatenate([x[:32], x[32:]], 1))
    return results


def swap_blocks(x):
    row = iota(x.shape, 0)
    block = iota(x.shape, 1) // 16
    for s in (1, 2, 4):
        row_bit = (row // s) % 2
        block_bit = (block // s) % 2
        up = pltpu.roll(pltpu.roll(x, 64 - s, 0), 16 * s, 1)
        down = pltpu.roll(pltpu.roll(x, s, 0), 128 - 16 * s, 1)
        x = jnp.where(row_bit == block_bit, x, jnp.where(row_bit < block_bit, up, down))
    return x


def offsets():
    every = [(z, x, c) for z in range(4) for x in range(4) for c in range(2) if z or x or c]
    return sorted(every, key=lambda o: (-(min(o[0], 4 - o[0]) + min(o[1], 4 - o[1])), o[2]))


def kernel(
    bg, value, height, obs_weight, index, counts, owner, table, out, load_recv,
    value_v, height_v, weight_v, index_v, counts_v, owner_v, table_v,
    message, received, fields, shared, load_send, rows_in, rows_out, rows_own,
    tile_ready, small_sem, stage_sem, in_send, in_recv, out_send, out_recv, obs_send, obs_recv, load_sems,
):
    me = lax.axis_index("mem")
    tile = lax.axis_index("tile")
    z, x, core = me // 8, (me // 2) % 4, me % 2
    zs = [lax.rem(z + d, 4) * 8 for d in range(4)]
    xs = [lax.rem(x + d, 4) * 2 for d in range(4)]
    cores = [core, 1 - core]
    partners = []
    for dz, dx, dc in offsets():
        chips = jnp.where(core == 0, zs[dz] + xs[dx], zs[-dx % 4] + xs[-dz % 4])
        partners.append(chips + cores[dc])
    tile_partners = [lax.rem(tile + d, N_TILE) for d in range(1, N_TILE)]
    small = [
        pltpu.make_async_copy(a, b, small_sem.at[i])
        for i, (a, b) in enumerate(
            zip(
                (value, height, obs_weight, index, counts, owner, table),
                (value_v, height_v, weight_v, index_v, counts_v, owner_v, table_v),
            )
        )
    ]
    for copy in small:
        copy.start()
    stage = pltpu.make_async_copy(bg, rows_own, stage_sem)
    stage.start()
    barrier = pltpu.get_barrier_semaphore()
    for p in partners:
        pl.semaphore_signal(barrier, inc=1, device_id=(p, tile), device_id_type=MESH)

    def greet(there, semaphore, q):
        @pl.when(there)
        def _():
            pl.semaphore_signal(semaphore, inc=1, device_id=(me, q), device_id_type=MESH)

    for q in tile_partners:
        greet(q > tile, barrier, q)
    for copy in small:
        copy.wait()

    localised = jnp.zeros((OBS_L, COLS_T), F32)
    entry = index_v[...]
    table_row = table_v[...]
    for k in range(LOC_N):
        localised = jnp.where(entry == k, table_row[:, k : k + 1], localised)
    live = (me * OBS_L + iota((OBS_L, COLS_T), 0)) < counts_v[...]
    weights = jnp.where(live, localised * weight_v[...], 0.0)
    first = jnp.concatenate([value_v[...], height_v[...]], 0)
    second = jnp.concatenate([weights, jnp.zeros((OBS_L, COLS_T), F32)], 0)
    stack = []
    for b in range(4):
        stack += [first[:, 128 * b : 128 * b + 128], second[:, 128 * b : 128 * b + 128]]
    stack = swap_blocks(jnp.concatenate(stack, 0))
    column_load = jnp.sum(weights, 0, keepdims=True)
    right_half = jnp.concatenate([stack[16 * b + 8 : 16 * b + 16] for b in range(4)], 0)
    lane = iota((N_MEM, 128), 1)
    first_owner = iota((N_MEM, COLS_T), 0) * N_TILE
    owners = owner_v[...]
    for q in range(N_TILE):
        part = jnp.sum(
            jnp.where(first_owner + q == owners, column_load, 0.0), 1, keepdims=True
        )
        right_half = jnp.where(lane == 64 + q, part, right_half)
    left_half = jnp.concatenate([stack[16 * b : 16 * b + 8] for b in range(4)], 0)
    message[...] = jnp.concatenate([left_half, right_half], 1).reshape(N_MEM, 1, WIDTH)

    def source(c, p):
        return rows_own.at[pl.ds(pl.multiple_of(p * OWN + c * CHUNK, CHUNK), CHUNK)]

    stage.wait()
    for c in range(CHUNKS):
        pltpu.make_async_copy(source(c, me), rows_in.at[c, me], in_recv.at[c]).start()
    pl.semaphore_wait(barrier, N_MEM - 1 + tile)

    def send_rows(c):
        for p in partners:
            pltpu.make_async_remote_copy(
                src_ref=source(c, p),
                dst_ref=rows_in.at[c, me],
                send_sem=in_send.at[c],
                recv_sem=in_recv.at[c],
                device_id=(p, tile),
                device_id_type=MESH,
            ).start()

    for p in partners:
        pltpu.make_async_remote_copy(
            src_ref=message.at[p],
            dst_ref=received.at[me],
            send_sem=obs_send,
            recv_sem=obs_recv,
            device_id=(p, tile),
            device_id_type=MESH,
        ).start()
    pltpu.make_async_copy(message.at[me], received.at[me], obs_recv).start()
    for c in range(CHUNKS):
        send_rows(c)

    for q in tile_partners:
        greet(q < tile, tile_ready, q)
    pltpu.make_async_copy(received, received, obs_recv).wait()
    arrived = received[...].reshape(N_MEM, WIDTH)
    arrived = jnp.concatenate([arrived, jnp.zeros((128 - N_MEM, WIDTH), F32)], 0).T
    for f in range(3):
        fields[f] = jnp.concatenate(
            [arrived[(4 * f + o) * OWN : (4 * f + o + 1) * OWN, :N_MEM] for o in range(OBS_L)], 1
        )
    loads = jnp.sum(arrived[192 : 192 + N_TILE], 1, keepdims=True)
    load_send[...] = jnp.broadcast_to(loads, (N_TILE, 128)).reshape(N_TILE, 1, 128)

    @pl.when(tile < N_TILE - 1)
    def _():
        pl.semaphore_wait(tile_ready, N_TILE - 1 - tile)

    for q in tile_partners:
        pltpu.make_async_remote_copy(
            src_ref=load_send.at[q],
            dst_ref=load_recv.at[tile],
            send_sem=load_sems.at[0],
            recv_sem=load_sems.at[1],
            device_id=(me, q),
            device_id_type=MESH,
        ).start()
    pltpu.make_async_copy(load_send.at[tile], load_recv.at[tile], load_sems.at[1]).start()

    observe(fields, shared)

    def step(c, carry):
        pltpu.make_async_copy(rows_in.at[c], rows_in.at[c], in_recv.at[c]).wait()
        results = analyse(
            [rows_in[c, :, i, :] for i in range(CHUNK)],
            [
                [shared[c * (CHUNK // 2) + q, k] for k in range(3)]
                for q in range(CHUNK // 2)
            ],
        )
        for i in range(CHUNK):
            rows_out[c, :, i, :] = results[i]
        target = out.at[pl.ds(pl.multiple_of(me * OWN + c * CHUNK, CHUNK), CHUNK)]

        def send_out(p):
            pltpu.make_async_remote_copy(
                src_ref=rows_out.at[c, p],
                dst_ref=target,
                send_sem=out_send.at[c],
                recv_sem=out_recv.at[c],
                device_id=(p, tile),
                device_id_type=MESH,
            ).start()

        for p in BY_START:
            pl.when(p != me)(functools.partial(send_out, p))
        pltpu.make_async_copy(rows_out.at[c, me], target, out_recv.at[c]).start()
        return carry

    lax.fori_loop(0, CHUNKS, step, 0)

    pltpu.make_async_copy(load_recv, load_recv, load_sems.at[1]).wait()
    sent = load_send.at[pl.ds(0, N_TILE - 1)]
    pltpu.make_async_copy(sent, sent, load_sems.at[0]).wait()
    sent = message.at[pl.ds(0, N_MEM - 1)]
    pltpu.make_async_copy(sent, sent, obs_send).wait()
    for c in range(CHUNKS):
        sent = rows_in.at[c, pl.ds(0, N_MEM - 1)]
        pltpu.make_async_copy(sent, sent, in_send.at[c]).wait()
        pltpu.make_async_copy(sent, sent, out_send.at[c]).wait()
        pltpu.make_async_copy(rows_out.at[c], rows_out.at[c], out_recv.at[c]).wait()


def finish(rows, parts, out, load_out, load_v, sems):
    rows_copy = pltpu.make_async_copy(rows, out, sems.at[0])
    rows_copy.start()
    load_v[...] = jnp.sum(parts[...], 0) * (1.0 / (OBS * CAP))
    load_copy = pltpu.make_async_copy(load_v, load_out, sems.at[1])
    load_copy.start()
    rows_copy.wait()
    load_copy.wait()


def per_device(background, obs_value, obs_height, obs_weight, counts, owner, loc_index, loc_table):
    hbm = pl.BlockSpec(memory_space=pl.ANY)

    def keep(x):
        return pltpu.with_memory_space_constraint(x, pltpu.HBM)

    dma = pltpu.SemaphoreType.DMA
    analysis, load = pl.pallas_call(
        kernel,
        out_shape=(
            jax.ShapeDtypeStruct((COLS_T, WIDTH), F32),
            jax.ShapeDtypeStruct((N_TILE, 1, 128), F32),
        ),
        in_specs=[hbm] * 8,
        out_specs=(hbm, hbm),
        scratch_shapes=[
            pltpu.VMEM((OBS_L, COLS_T), F32),
            pltpu.VMEM((OBS_L, COLS_T), F32),
            pltpu.VMEM((OBS_L, COLS_T), F32),
            pltpu.VMEM((OBS_L, COLS_T), jnp.int32),
            pltpu.VMEM((1, COLS_T), jnp.int32),
            pltpu.VMEM((1, COLS_T), jnp.int32),
            pltpu.VMEM((1, LOC_N), F32),
            pltpu.VMEM((N_MEM, 1, WIDTH), F32),
            pltpu.VMEM((N_MEM, 1, WIDTH), F32),
            pltpu.VMEM((3, OWN, OBS), F32),
            pltpu.VMEM((OWN // 2, 3, 64, 128), F32),
            pltpu.VMEM((N_TILE, 1, 128), F32),
            pltpu.VMEM((CHUNKS, N_MEM, CHUNK, WIDTH), F32),
            pltpu.VMEM((CHUNKS, N_MEM, CHUNK, WIDTH), F32),
            pltpu.VMEM((COLS_T, WIDTH), F32),
            pltpu.SemaphoreType.REGULAR,
            dma((7,)),
            dma,
            dma((CHUNKS,)),
            dma((CHUNKS,)),
            dma((CHUNKS,)),
            dma((CHUNKS,)),
            dma,
            dma,
            dma((2,)),
        ],
        compiler_params=pltpu.CompilerParams(
            collective_id=0, has_side_effects=True, vmem_limit_bytes=16 << 20
        ),
    )(
        keep(background),
        keep(obs_value.T),
        keep(obs_height.T),
        keep(obs_weight.T),
        keep(loc_index.T),
        keep(counts.reshape(1, COLS_T)),
        keep(owner.reshape(1, COLS_T)),
        keep(loc_table.reshape(1, LOC_N)),
    )
    analysis, load = pl.pallas_call(
        finish,
        out_shape=(
            jax.ShapeDtypeStruct((COLS_T, WIDTH), F32),
            jax.ShapeDtypeStruct((1, 128), F32),
        ),
        in_specs=[hbm, pl.BlockSpec(memory_space=pltpu.VMEM)],
        out_specs=(hbm, hbm),
        scratch_shapes=[pltpu.VMEM((1, 128), F32), dma((2,))],
        compiler_params=pltpu.CompilerParams(vmem_limit_bytes=16 << 20),
    )(analysis, load)
    return analysis, load[0, :1]


def solution(mesh):
    placed = (
        P("tile", "mem"),
        P("tile", "mem"),
        P("tile", "mem"),
        P("tile", "mem"),
        P("tile"),
        P("tile", None),
        P("tile", "mem"),
        P(),
    )
    return jax.shard_map(
        per_device,
        mesh=mesh,
        in_specs=placed,
        out_specs=(P("tile", "mem"), P(("mem", "tile"))),
        check_vma=False,
    )
```

```python
import functools

import jax
import jax.numpy as jnp
from jax import lax
from jax.experimental import pallas as pl
from jax.experimental.pallas import tpu as pltpu
from jax.sharding import PartitionSpec as P

LEV = 64
OBS = 128
LOC_N = 16
CAP = 8
N_MEM = 32
N_TILE = 4
COLS_T = 512
OWN = COLS_T // N_MEM
CHUNK = 8
CHUNKS = OWN // CHUNK
OBS_L = OBS // N_MEM
WIDTH = 256
BY_START = [
    2 * chip + core
    for chip in sorted(range(N_MEM // 2), key=lambda k: 1.1 * (k // 4) + 0.45 * (k % 4))
    for core in (1, 0)
]

F32 = jnp.float32
BF16 = jnp.bfloat16
MESH = pl.DeviceIdType.MESH


def iota(shape, axis):
    return lax.broadcasted_iota(jnp.int32, shape, axis)


def split(x):
    high = x.astype(BF16)
    return high, (x - high.astype(F32)).astype(BF16)


def right_side(x, keep0, keep1):
    high, low = split(x)
    top = jnp.concatenate([high * keep0, low * keep0], 1)
    bottom = jnp.concatenate([high * keep1, low * keep1], 1)
    return jnp.concatenate([top, bottom, top, bottom], 0)


def product(a, right):
    high, low = split(a)
    both = jnp.dot(jnp.concatenate([high, low], 1), right, preferred_element_type=F32)
    return both[:, :128] + both[:, 128:]


def lane_masks():
    lane = iota((64, 128), 1)
    left = lane < 64
    keep0 = jnp.where(left, 1.0, 0.0).astype(BF16)
    keep1 = jnp.where(left, 0.0, 1.0).astype(BF16)
    return lane, iota((64, 128), 0), left, keep0, keep1


def observe(fields, shared):
    left = lane_masks()[2]
    level = iota((64, 128), 0).astype(F32)

    def pair(q, carry):
        both = []
        for j in (0, 1):
            value, height, weight = [fields[f, pl.ds(2 * q + j, 1), :] for f in range(3)]
            hat = jnp.maximum(0.0, 1.0 - jnp.abs(level - height))
            hat_next = jnp.maximum(0.0, 1.0 - jnp.abs((level + 1.0) - height))
            weighted = weight * hat
            terms = (weighted * hat, weighted * hat_next, weighted * value)
            both.append([jnp.sum(x, 1, keepdims=True) for x in terms])
        for k in range(3):
            shared[q, k] = jnp.where(left, both[0][k], both[1][k])
        return carry

    lax.fori_loop(0, OWN // 2, pair, 0, unroll=8)


def analyse(blocks, shared):
    lane, row, left, keep0, keep1 = lane_masks()
    left1 = left[:1]
    eye = jnp.where((lane & 63) == row, 1.0, 0.0)
    pairs = range(len(shared))

    def exchange(x, y):
        return jnp.where(left, x, pltpu.roll(y, 64, 1)), jnp.where(left, pltpu.roll(x, 64, 1), y)

    halves, centre, square, mean_col = [], [], [], []
    for q in pairs:
        x, y = [jnp.concatenate([b[:, :128], b[:, 128:]], 0) for b in blocks[2 * q : 2 * q + 2]]
        x = jnp.concatenate(exchange(x, y), 0)
        mean = jnp.sum(x, 0, keepdims=True) * (1.0 / 128.0)
        high, low = split(x - mean)
        both = lax.dot_general(
            jnp.concatenate([high, low], 0),
            jnp.concatenate([jnp.concatenate([high, low], 1)] * 2, 0),
            (((0,), (0,)), ((), ())),
            preferred_element_type=F32,
        )
        square.append(both[:, :128] + both[:, 128:])
        diagonal = eye * mean
        mean_col.append(
            jnp.where(
                left,
                jnp.sum(jnp.where(left, diagonal, 0.0), 1, keepdims=True),
                jnp.sum(jnp.where(left, 0.0, diagonal), 1, keepdims=True),
            )
        )
        halves.append(jnp.concatenate([high, low], 1))
        centre.append(mean)
    base, force = [], []
    for q in pairs:
        g = jnp.where(left, square[q][:64], square[q][64:])
        d, e, w = shared[q]

        def tridiagonal(m):
            return d * m + pltpu.roll(e * m, 1, 0) + e * pltpu.roll(m, 63, 0)

        w = w - tridiagonal(mean_col[q])
        base.append(tridiagonal(g))
        force.append(jnp.broadcast_to(jnp.sum(w * g, 0, keepdims=True), (16, 128)))
    right = [right_side(b, keep0, keep1) for b in base]
    out = [product(jnp.concatenate([base[q], force[q]], 0), right[q]) for q in pairs]
    cube = [product(out[q][:64], right[q]) for q in pairs]
    p, z, t, inverse = [], [], [], []
    for q in pairs:
        b, b2 = base[q], out[q][:64]
        trace = jnp.sum(eye * (254.0 * b + b2), 0, keepdims=True)
        norm2 = 127.0 * 127.0 * 128.0 + jnp.where(
            left1,
            jnp.sum(jnp.where(left1, trace, 0.0), 1, keepdims=True),
            jnp.sum(jnp.where(left1, 0.0, trace), 1, keepdims=True),
        )
        a = lax.rsqrt(norm2)
        u = 127.0 * a
        p.append(
            (u * (2.25 + u * (-1.5 + 0.25 * u))) * eye
            + (a * (2.25 + u * (-3.0 + 0.75 * u))) * b
            + (a * a * (-1.5 + 0.75 * u)) * b2
            + (a * a * a * 0.25) * cube[q]
        )
        z.append((1.5 - 0.5 * u) * eye - (0.5 * a) * b)
        t.append((1.5 - 0.5 * u) * force[q] - (0.5 * a) * out[q][64:])
        inverse.append(a)
    for sweep in range(3):
        right = [right_side(p[q], keep0, keep1) for q in pairs]
        out = [product(jnp.concatenate([p[q], z[q], t[q]], 0), right[q]) for q in pairs]
        cube = [product(out[q][:64], right[q]) for q in pairs]
        for q in pairs:
            z[q] = 1.5 * z[q] - 0.5 * out[q][64:128]
            t[q] = 1.5 * t[q] - 0.5 * out[q][128:]
            p[q] = 2.25 * p[q] - 1.5 * out[q][:64] + 0.25 * cube[q]
    results = []
    for q in pairs:
        out = product(jnp.concatenate([z[q], t[q]], 0), right_side(p[q], keep0, keep1))
        z[q] = 1.5 * z[q] - 0.5 * out[:64]
        t[q] = 1.5 * t[q] - 0.5 * out[64:]
    for q in pairs:
        t_halves = jnp.concatenate(split(t[q]), 1)
        both = jnp.dot(
            jnp.concatenate([halves[q], t_halves], 0),
            right_side(z[q], keep0, keep1),
            preferred_element_type=F32,
        )
        both = both[:, :128] + both[:, 128:]
        full = (centre[q] + inverse[q] * both[128:129]) + jnp.sqrt(127.0 * inverse[q]) * both[:128]
        for x in exchange(full[:64], full[64:]):
            results.append(jnp.concatenate([x[:32], x[32:]], 1))
    return results


def swap_blocks(x):
    row = iota(x.shape, 0)
    block = iota(x.shape, 1) // 16
    for s in (1, 2, 4):
        row_bit = (row // s) % 2
        block_bit = (block // s) % 2
        up = pltpu.roll(pltpu.roll(x, 64 - s, 0), 16 * s, 1)
        down = pltpu.roll(pltpu.roll(x, s, 0), 128 - 16 * s, 1)
        x = jnp.where(row_bit == block_bit, x, jnp.where(row_bit < block_bit, up, down))
    return x


def offsets():
    every = [(z, x, c) for z in range(4) for x in range(4) for c in range(2) if z or x or c]
    return sorted(every, key=lambda o: (-(min(o[0], 4 - o[0]) + min(o[1], 4 - o[1])), o[2]))


def kernel(
    bg, value, height, obs_weight, index, counts, owner, table, out, load_recv,
    value_v, height_v, weight_v, index_v, counts_v, owner_v, table_v,
    message, received, fields, shared, load_send, rows_in, rows_out, rows_own,
    tile_ready, small_sem, stage_sem, in_send, in_recv, out_send, out_recv, obs_send, obs_recv, load_sems,
):
    me = lax.axis_index("mem")
    tile = lax.axis_index("tile")
    z, x, core = me // 8, (me // 2) % 4, me % 2
    zs = [lax.rem(z + d, 4) * 8 for d in range(4)]
    xs = [lax.rem(x + d, 4) * 2 for d in range(4)]
    cores = [core, 1 - core]
    partners = []
    for dz, dx, dc in offsets():
        chips = jnp.where(core == 0, zs[dz] + xs[dx], zs[-dx % 4] + xs[-dz % 4])
        partners.append(chips + cores[dc])
    tile_partners = [lax.rem(tile + d, N_TILE) for d in range(1, N_TILE)]
    small = [
        pltpu.make_async_copy(a, b, small_sem.at[i])
        for i, (a, b) in enumerate(
            zip(
                (value, height, obs_weight, index, counts, owner, table),
                (value_v, height_v, weight_v, index_v, counts_v, owner_v, table_v),
            )
        )
    ]
    for copy in small:
        copy.start()
    stage = pltpu.make_async_copy(bg, rows_own, stage_sem)
    stage.start()
    barrier = pltpu.get_barrier_semaphore()
    for p in partners:
        pl.semaphore_signal(barrier, inc=1, device_id=(p, tile), device_id_type=MESH)

    def greet(there, semaphore, q):
        @pl.when(there)
        def _():
            pl.semaphore_signal(semaphore, inc=1, device_id=(me, q), device_id_type=MESH)

    for q in tile_partners:
        greet(q > tile, barrier, q)
    for copy in small:
        copy.wait()

    localised = jnp.zeros((OBS_L, COLS_T), F32)
    entry = index_v[...]
    table_row = table_v[...]
    for k in range(LOC_N):
        localised = jnp.where(entry == k, table_row[:, k : k + 1], localised)
    live = (me * OBS_L + iota((OBS_L, COLS_T), 0)) < counts_v[...]
    weights = jnp.where(live, localised * weight_v[...], 0.0)
    first = jnp.concatenate([value_v[...], height_v[...]], 0)
    second = jnp.concatenate([weights, jnp.zeros((OBS_L, COLS_T), F32)], 0)
    stack = []
    for b in range(4):
        stack += [first[:, 128 * b : 128 * b + 128], second[:, 128 * b : 128 * b + 128]]
    stack = swap_blocks(jnp.concatenate(stack, 0))
    column_load = jnp.sum(weights, 0, keepdims=True)
    right_half = jnp.concatenate([stack[16 * b + 8 : 16 * b + 16] for b in range(4)], 0)
    lane = iota((N_MEM, 128), 1)
    first_owner = iota((N_MEM, COLS_T), 0) * N_TILE
    owners = owner_v[...]
    for q in range(N_TILE):
        part = jnp.sum(
            jnp.where(first_owner + q == owners, column_load, 0.0), 1, keepdims=True
        )
        right_half = jnp.where(lane == 64 + q, part, right_half)
    left_half = jnp.concatenate([stack[16 * b : 16 * b + 8] for b in range(4)], 0)
    message[...] = jnp.concatenate([left_half, right_half], 1).reshape(N_MEM, 1, WIDTH)

    def source(c, p):
        return rows_own.at[pl.ds(pl.multiple_of(p * OWN + c * CHUNK, CHUNK), CHUNK)]

    stage.wait()
    for c in range(CHUNKS):
        pltpu.make_async_copy(source(c, me), rows_in.at[c, me], in_recv.at[c]).start()
    pl.semaphore_wait(barrier, N_MEM - 1 + tile)

    def send_rows(c):
        for p in partners:
            pltpu.make_async_remote_copy(
                src_ref=source(c, p),
                dst_ref=rows_in.at[c, me],
                send_sem=in_send.at[c],
                recv_sem=in_recv.at[c],
                device_id=(p, tile),
                device_id_type=MESH,
            ).start()

    for p in partners:
        pltpu.make_async_remote_copy(
            src_ref=message.at[p],
            dst_ref=received.at[me],
            send_sem=obs_send,
            recv_sem=obs_recv,
            device_id=(p, tile),
            device_id_type=MESH,
        ).start()
    pltpu.make_async_copy(message.at[me], received.at[me], obs_recv).start()
    for c in range(CHUNKS):
        send_rows(c)

    for q in tile_partners:
        greet(q < tile, tile_ready, q)
    pltpu.make_async_copy(received, received, obs_recv).wait()
    arrived = received[...].reshape(N_MEM, WIDTH)
    arrived = jnp.concatenate([arrived, jnp.zeros((128 - N_MEM, WIDTH), F32)], 0).T
    for f in range(3):
        fields[f] = jnp.concatenate(
            [arrived[(4 * f + o) * OWN : (4 * f + o + 1) * OWN, :N_MEM] for o in range(OBS_L)], 1
        )
    observe(fields, shared)

    def step(c, carry):
        pltpu.make_async_copy(rows_in.at[c], rows_in.at[c], in_recv.at[c]).wait()
        results = analyse(
            [rows_in[c, :, i, :] for i in range(CHUNK)],
            [
                [shared[c * (CHUNK // 2) + q, k] for k in range(3)]
                for q in range(CHUNK // 2)
            ],
        )
        for i in range(CHUNK):
            rows_out[c, :, i, :] = results[i]
        target = out.at[pl.ds(pl.multiple_of(me * OWN + c * CHUNK, CHUNK), CHUNK)]

        def send_out(p):
            pltpu.make_async_remote_copy(
                src_ref=rows_out.at[c, p],
                dst_ref=target,
                send_sem=out_send.at[c],
                recv_sem=out_recv.at[c],
                device_id=(p, tile),
                device_id_type=MESH,
            ).start()

        for p in BY_START:
            pl.when(p != me)(functools.partial(send_out, p))
        pltpu.make_async_copy(rows_out.at[c, me], target, out_recv.at[c]).start()
        return carry

    kept = jnp.sum(arrived[192 : 192 + N_TILE], 1, keepdims=True)
    for c in range(CHUNKS):
        step(c, 0)
        if c == 0:
            loads = kept
            load_send[...] = jnp.broadcast_to(loads, (N_TILE, 128)).reshape(N_TILE, 1, 128)

            @pl.when(tile < N_TILE - 1)
            def _():
                pl.semaphore_wait(tile_ready, N_TILE - 1 - tile)

            for q in tile_partners:
                pltpu.make_async_remote_copy(
                    src_ref=load_send.at[q],
                    dst_ref=load_recv.at[tile],
                    send_sem=load_sems.at[0],
                    recv_sem=load_sems.at[1],
                    device_id=(me, q),
                    device_id_type=MESH,
                ).start()
            pltpu.make_async_copy(load_send.at[tile], load_recv.at[tile], load_sems.at[1]).start()


    pltpu.make_async_copy(load_recv, load_recv, load_sems.at[1]).wait()
    sent = load_send.at[pl.ds(0, N_TILE - 1)]
    pltpu.make_async_copy(sent, sent, load_sems.at[0]).wait()
    sent = message.at[pl.ds(0, N_MEM - 1)]
    pltpu.make_async_copy(sent, sent, obs_send).wait()
    for c in range(CHUNKS):
        sent = rows_in.at[c, pl.ds(0, N_MEM - 1)]
        pltpu.make_async_copy(sent, sent, in_send.at[c]).wait()
        pltpu.make_async_copy(sent, sent, out_send.at[c]).wait()
        pltpu.make_async_copy(rows_out.at[c], rows_out.at[c], out_recv.at[c]).wait()


def finish(rows, parts, out, load_out, load_v, sems):
    rows_copy = pltpu.make_async_copy(rows, out, sems.at[0])
    rows_copy.start()
    load_v[...] = jnp.sum(parts[...], 0) * (1.0 / (OBS * CAP))
    load_copy = pltpu.make_async_copy(load_v, load_out, sems.at[1])
    load_copy.start()
    rows_copy.wait()
    load_copy.wait()


def per_device(background, obs_value, obs_height, obs_weight, counts, owner, loc_index, loc_table):
    hbm = pl.BlockSpec(memory_space=pl.ANY)

    def keep(x):
        return pltpu.with_memory_space_constraint(x, pltpu.HBM)

    dma = pltpu.SemaphoreType.DMA
    analysis, load = pl.pallas_call(
        kernel,
        out_shape=(
            jax.ShapeDtypeStruct((COLS_T, WIDTH), F32),
            jax.ShapeDtypeStruct((N_TILE, 1, 128), F32),
        ),
        in_specs=[hbm] * 8,
        out_specs=(hbm, hbm),
        scratch_shapes=[
            pltpu.VMEM((OBS_L, COLS_T), F32),
            pltpu.VMEM((OBS_L, COLS_T), F32),
            pltpu.VMEM((OBS_L, COLS_T), F32),
            pltpu.VMEM((OBS_L, COLS_T), jnp.int32),
            pltpu.VMEM((1, COLS_T), jnp.int32),
            pltpu.VMEM((1, COLS_T), jnp.int32),
            pltpu.VMEM((1, LOC_N), F32),
            pltpu.VMEM((N_MEM, 1, WIDTH), F32),
            pltpu.VMEM((N_MEM, 1, WIDTH), F32),
            pltpu.VMEM((3, OWN, OBS), F32),
            pltpu.VMEM((OWN // 2, 3, 64, 128), F32),
            pltpu.VMEM((N_TILE, 1, 128), F32),
            pltpu.VMEM((CHUNKS, N_MEM, CHUNK, WIDTH), F32),
            pltpu.VMEM((CHUNKS, N_MEM, CHUNK, WIDTH), F32),
            pltpu.VMEM((COLS_T, WIDTH), F32),
            pltpu.SemaphoreType.REGULAR,
            dma((7,)),
            dma,
            dma((CHUNKS,)),
            dma((CHUNKS,)),
            dma((CHUNKS,)),
            dma((CHUNKS,)),
            dma,
            dma,
            dma((2,)),
        ],
        compiler_params=pltpu.CompilerParams(
            collective_id=0, has_side_effects=True, vmem_limit_bytes=16 << 20
        ),
    )(
        keep(background),
        keep(obs_value.T),
        keep(obs_height.T),
        keep(obs_weight.T),
        keep(loc_index.T),
        keep(counts.reshape(1, COLS_T)),
        keep(owner.reshape(1, COLS_T)),
        keep(loc_table.reshape(1, LOC_N)),
    )
    analysis, load = pl.pallas_call(
        finish,
        out_shape=(
            jax.ShapeDtypeStruct((COLS_T, WIDTH), F32),
            jax.ShapeDtypeStruct((1, 128), F32),
        ),
        in_specs=[hbm, pl.BlockSpec(memory_space=pltpu.VMEM)],
        out_specs=(hbm, hbm),
        scratch_shapes=[pltpu.VMEM((1, 128), F32), dma((2,))],
        compiler_params=pltpu.CompilerParams(vmem_limit_bytes=16 << 20),
    )(analysis, load)
    return analysis, load[0, :1]


def solution(mesh):
    placed = (
        P("tile", "mem"),
        P("tile", "mem"),
        P("tile", "mem"),
        P("tile", "mem"),
        P("tile"),
        P("tile", None),
        P("tile", "mem"),
        P(),
    )
    return jax.shard_map(
        per_device,
        mesh=mesh,
        in_specs=placed,
        out_specs=(P("tile", "mem"), P(("mem", "tile"))),
        check_vma=False,
    )
```

```python
import functools

import jax
import jax.numpy as jnp
from jax import lax
from jax.experimental import pallas as pl
from jax.experimental.pallas import tpu as pltpu
from jax.sharding import PartitionSpec as P

LEV = 64
OBS = 128
LOC_N = 16
CAP = 8
N_MEM = 32
N_TILE = 4
COLS_T = 512
OWN = COLS_T // N_MEM
CHUNK = 8
CHUNKS = OWN // CHUNK
OBS_L = OBS // N_MEM
WIDTH = 256
BY_START = [
    2 * chip + core
    for chip in sorted(range(N_MEM // 2), key=lambda k: 1.1 * (k // 4) + 0.45 * (k % 4))
    for core in (1, 0)
]

F32 = jnp.float32
BF16 = jnp.bfloat16
MESH = pl.DeviceIdType.MESH


def iota(shape, axis):
    return lax.broadcasted_iota(jnp.int32, shape, axis)


def split(x):
    high = x.astype(BF16)
    return high, (x - high.astype(F32)).astype(BF16)


def right_side(x, keep0, keep1):
    high, low = split(x)
    top = jnp.concatenate([high * keep0, low * keep0], 1)
    bottom = jnp.concatenate([high * keep1, low * keep1], 1)
    return jnp.concatenate([top, bottom, top, bottom], 0)


def product(a, right):
    high, low = split(a)
    both = jnp.dot(jnp.concatenate([high, low], 1), right, preferred_element_type=F32)
    return both[:, :128] + both[:, 128:]


def lane_masks():
    lane = iota((64, 128), 1)
    left = lane < 64
    keep0 = jnp.where(left, 1.0, 0.0).astype(BF16)
    keep1 = jnp.where(left, 0.0, 1.0).astype(BF16)
    return lane, iota((64, 128), 0), left, keep0, keep1


def observe(fields, shared, first, count):
    left = lane_masks()[2]
    level = iota((64, 128), 0).astype(F32)

    def pair(q, carry):
        both = []
        for j in (0, 1):
            value, height, weight = [fields[f, pl.ds(2 * q + j, 1), :] for f in range(3)]
            hat = jnp.maximum(0.0, 1.0 - jnp.abs(level - height))
            hat_next = jnp.maximum(0.0, 1.0 - jnp.abs((level + 1.0) - height))
            weighted = weight * hat
            terms = (weighted * hat, weighted * hat_next, weighted * value)
            both.append([jnp.sum(x, 1, keepdims=True) for x in terms])
        for k in range(3):
            shared[q, k] = jnp.where(left, both[0][k], both[1][k])
        return carry

    for q in range(first, first + count):
        pair(q, 0)


def analyse(blocks, shared):
    lane, row, left, keep0, keep1 = lane_masks()
    left1 = left[:1]
    eye = jnp.where((lane & 63) == row, 1.0, 0.0)
    pairs = range(len(shared))

    def exchange(x, y):
        return jnp.where(left, x, pltpu.roll(y, 64, 1)), jnp.where(left, pltpu.roll(x, 64, 1), y)

    halves, centre, square, mean_col = [], [], [], []
    for q in pairs:
        x, y = [jnp.concatenate([b[:, :128], b[:, 128:]], 0) for b in blocks[2 * q : 2 * q + 2]]
        x = jnp.concatenate(exchange(x, y), 0)
        mean = jnp.sum(x, 0, keepdims=True) * (1.0 / 128.0)
        high, low = split(x - mean)
        both = lax.dot_general(
            jnp.concatenate([high, low], 0),
            jnp.concatenate([jnp.concatenate([high, low], 1)] * 2, 0),
            (((0,), (0,)), ((), ())),
            preferred_element_type=F32,
        )
        square.append(both[:, :128] + both[:, 128:])
        diagonal = eye * mean
        mean_col.append(
            jnp.where(
                left,
                jnp.sum(jnp.where(left, diagonal, 0.0), 1, keepdims=True),
                jnp.sum(jnp.where(left, 0.0, diagonal), 1, keepdims=True),
            )
        )
        halves.append(jnp.concatenate([high, low], 1))
        centre.append(mean)
    base, force = [], []
    for q in pairs:
        g = jnp.where(left, square[q][:64], square[q][64:])
        d, e, w = shared[q]

        def tridiagonal(m):
            return d * m + pltpu.roll(e * m, 1, 0) + e * pltpu.roll(m, 63, 0)

        w = w - tridiagonal(mean_col[q])
        base.append(tridiagonal(g))
        force.append(jnp.broadcast_to(jnp.sum(w * g, 0, keepdims=True), (16, 128)))
    right = [right_side(b, keep0, keep1) for b in base]
    out = [product(jnp.concatenate([base[q], force[q]], 0), right[q]) for q in pairs]
    cube = [product(out[q][:64], right[q]) for q in pairs]
    p, z, t, inverse = [], [], [], []
    for q in pairs:
        b, b2 = base[q], out[q][:64]
        trace = jnp.sum(eye * (254.0 * b + b2), 0, keepdims=True)
        norm2 = 127.0 * 127.0 * 128.0 + jnp.where(
            left1,
            jnp.sum(jnp.where(left1, trace, 0.0), 1, keepdims=True),
            jnp.sum(jnp.where(left1, 0.0, trace), 1, keepdims=True),
        )
        a = lax.rsqrt(norm2)
        u = 127.0 * a
        p.append(
            (u * (2.25 + u * (-1.5 + 0.25 * u))) * eye
            + (a * (2.25 + u * (-3.0 + 0.75 * u))) * b
            + (a * a * (-1.5 + 0.75 * u)) * b2
            + (a * a * a * 0.25) * cube[q]
        )
        z.append((1.5 - 0.5 * u) * eye - (0.5 * a) * b)
        t.append((1.5 - 0.5 * u) * force[q] - (0.5 * a) * out[q][64:])
        inverse.append(a)
    for sweep in range(3):
        right = [right_side(p[q], keep0, keep1) for q in pairs]
        out = [product(jnp.concatenate([p[q], z[q], t[q]], 0), right[q]) for q in pairs]
        cube = [product(out[q][:64], right[q]) for q in pairs]
        for q in pairs:
            z[q] = 1.5 * z[q] - 0.5 * out[q][64:128]
            t[q] = 1.5 * t[q] - 0.5 * out[q][128:]
            p[q] = 2.25 * p[q] - 1.5 * out[q][:64] + 0.25 * cube[q]
    results = []
    for q in pairs:
        out = product(jnp.concatenate([z[q], t[q]], 0), right_side(p[q], keep0, keep1))
        z[q] = 1.5 * z[q] - 0.5 * out[:64]
        t[q] = 1.5 * t[q] - 0.5 * out[64:]
    for q in pairs:
        t_halves = jnp.concatenate(split(t[q]), 1)
        both = jnp.dot(
            jnp.concatenate([halves[q], t_halves], 0),
            right_side(z[q], keep0, keep1),
            preferred_element_type=F32,
        )
        both = both[:, :128] + both[:, 128:]
        full = (centre[q] + inverse[q] * both[128:129]) + jnp.sqrt(127.0 * inverse[q]) * both[:128]
        for x in exchange(full[:64], full[64:]):
            results.append(jnp.concatenate([x[:32], x[32:]], 1))
    return results


def swap_blocks(x):
    row = iota(x.shape, 0)
    block = iota(x.shape, 1) // 16
    for s in (1, 2, 4):
        row_bit = (row // s) % 2
        block_bit = (block // s) % 2
        up = pltpu.roll(pltpu.roll(x, 64 - s, 0), 16 * s, 1)
        down = pltpu.roll(pltpu.roll(x, s, 0), 128 - 16 * s, 1)
        x = jnp.where(row_bit == block_bit, x, jnp.where(row_bit < block_bit, up, down))
    return x


def offsets():
    every = [(z, x, c) for z in range(4) for x in range(4) for c in range(2) if z or x or c]
    return sorted(every, key=lambda o: (-(min(o[0], 4 - o[0]) + min(o[1], 4 - o[1])), o[2]))


def kernel(
    bg, value, height, obs_weight, index, counts, owner, table, out, load_recv,
    value_v, height_v, weight_v, index_v, counts_v, owner_v, table_v,
    message, received, fields, shared, load_send, rows_in, rows_out, rows_own,
    tile_ready, small_sem, stage_sem, in_send, in_recv, out_send, out_recv, obs_send, obs_recv, load_sems,
):
    me = lax.axis_index("mem")
    tile = lax.axis_index("tile")
    z, x, core = me // 8, (me // 2) % 4, me % 2
    zs = [lax.rem(z + d, 4) * 8 for d in range(4)]
    xs = [lax.rem(x + d, 4) * 2 for d in range(4)]
    cores = [core, 1 - core]
    partners = []
    for dz, dx, dc in offsets():
        chips = jnp.where(core == 0, zs[dz] + xs[dx], zs[-dx % 4] + xs[-dz % 4])
        partners.append(chips + cores[dc])
    tile_partners = [lax.rem(tile + d, N_TILE) for d in range(1, N_TILE)]
    small = [
        pltpu.make_async_copy(a, b, small_sem.at[i])
        for i, (a, b) in enumerate(
            zip(
                (value, height, obs_weight, index, counts, owner, table),
                (value_v, height_v, weight_v, index_v, counts_v, owner_v, table_v),
            )
        )
    ]
    for copy in small:
        copy.start()
    stage = pltpu.make_async_copy(bg, rows_own, stage_sem)
    stage.start()
    barrier = pltpu.get_barrier_semaphore()
    for p in partners:
        pl.semaphore_signal(barrier, inc=1, device_id=(p, tile), device_id_type=MESH)

    def greet(there, semaphore, q):
        @pl.when(there)
        def _():
            pl.semaphore_signal(semaphore, inc=1, device_id=(me, q), device_id_type=MESH)

    for q in tile_partners:
        greet(q > tile, barrier, q)
    for copy in small:
        copy.wait()

    localised = jnp.zeros((OBS_L, COLS_T), F32)
    entry = index_v[...]
    table_row = table_v[...]
    for k in range(LOC_N):
        localised = jnp.where(entry == k, table_row[:, k : k + 1], localised)
    live = (me * OBS_L + iota((OBS_L, COLS_T), 0)) < counts_v[...]
    weights = jnp.where(live, localised * weight_v[...], 0.0)
    first = jnp.concatenate([value_v[...], height_v[...]], 0)
    second = jnp.concatenate([weights, jnp.zeros((OBS_L, COLS_T), F32)], 0)
    stack = []
    for b in range(4):
        stack += [first[:, 128 * b : 128 * b + 128], second[:, 128 * b : 128 * b + 128]]
    stack = swap_blocks(jnp.concatenate(stack, 0))
    column_load = jnp.sum(weights, 0, keepdims=True)
    right_half = jnp.concatenate([stack[16 * b + 8 : 16 * b + 16] for b in range(4)], 0)
    lane = iota((N_MEM, 128), 1)
    first_owner = iota((N_MEM, COLS_T), 0) * N_TILE
    owners = owner_v[...]
    for q in range(N_TILE):
        part = jnp.sum(
            jnp.where(first_owner + q == owners, column_load, 0.0), 1, keepdims=True
        )
        right_half = jnp.where(lane == 64 + q, part, right_half)
    left_half = jnp.concatenate([stack[16 * b : 16 * b + 8] for b in range(4)], 0)
    message[...] = jnp.concatenate([left_half, right_half], 1).reshape(N_MEM, 1, WIDTH)

    def source(c, p):
        return rows_own.at[pl.ds(pl.multiple_of(p * OWN + c * CHUNK, CHUNK), CHUNK)]

    stage.wait()
    for c in range(CHUNKS):
        pltpu.make_async_copy(source(c, me), rows_in.at[c, me], in_recv.at[c]).start()
    pl.semaphore_wait(barrier, N_MEM - 1 + tile)

    def send_rows(c):
        for p in partners:
            pltpu.make_async_remote_copy(
                src_ref=source(c, p),
                dst_ref=rows_in.at[c, me],
                send_sem=in_send.at[c],
                recv_sem=in_recv.at[c],
                device_id=(p, tile),
                device_id_type=MESH,
            ).start()

    for p in partners:
        pltpu.make_async_remote_copy(
            src_ref=message.at[p],
            dst_ref=received.at[me],
            send_sem=obs_send,
            recv_sem=obs_recv,
            device_id=(p, tile),
            device_id_type=MESH,
        ).start()
    pltpu.make_async_copy(message.at[me], received.at[me], obs_recv).start()
    for c in range(CHUNKS):
        send_rows(c)

    for q in tile_partners:
        greet(q < tile, tile_ready, q)
    pltpu.make_async_copy(received, received, obs_recv).wait()
    arrived = received[...].reshape(N_MEM, WIDTH)
    arrived = arrived.T
    for f in range(3):
        fields[f] = jnp.concatenate(
            [arrived[(4 * f + o) * OWN : (4 * f + o + 1) * OWN, :N_MEM] for o in range(OBS_L)], 1
        )
    observe(fields, shared, 0, CHUNK // 2)

    def step(c, carry):
        pltpu.make_async_copy(rows_in.at[c], rows_in.at[c], in_recv.at[c]).wait()
        results = analyse(
            [rows_in[c, :, i, :] for i in range(CHUNK)],
            [
                [shared[c * (CHUNK // 2) + q, k] for k in range(3)]
                for q in range(CHUNK // 2)
            ],
        )
        if c + 1 < CHUNKS:
            observe(fields, shared, (c + 1) * (CHUNK // 2), CHUNK // 2)
        for i in range(CHUNK):
            rows_out[c, :, i, :] = results[i]
        target = out.at[pl.ds(pl.multiple_of(me * OWN + c * CHUNK, CHUNK), CHUNK)]

        def send_out(p):
            pltpu.make_async_remote_copy(
                src_ref=rows_out.at[c, p],
                dst_ref=target,
                send_sem=out_send.at[c],
                recv_sem=out_recv.at[c],
                device_id=(p, tile),
                device_id_type=MESH,
            ).start()

        for p in BY_START:
            pl.when(p != me)(functools.partial(send_out, p))
        pltpu.make_async_copy(rows_out.at[c, me], target, out_recv.at[c]).start()
        return carry

    kept = jnp.sum(arrived[192 : 192 + N_TILE], 1, keepdims=True)
    for c in range(CHUNKS):
        step(c, 0)
        if c == 0:
            loads = kept
            load_send[...] = jnp.broadcast_to(loads, (N_TILE, 128)).reshape(N_TILE, 1, 128)

            @pl.when(tile < N_TILE - 1)
            def _():
                pl.semaphore_wait(tile_ready, N_TILE - 1 - tile)

            for q in tile_partners:
                pltpu.make_async_remote_copy(
                    src_ref=load_send.at[q],
                    dst_ref=load_recv.at[tile],
                    send_sem=load_sems.at[0],
                    recv_sem=load_sems.at[1],
                    device_id=(me, q),
                    device_id_type=MESH,
                ).start()
            pltpu.make_async_copy(load_send.at[tile], load_recv.at[tile], load_sems.at[1]).start()


    pltpu.make_async_copy(load_recv, load_recv, load_sems.at[1]).wait()
    sent = load_send.at[pl.ds(0, N_TILE - 1)]
    pltpu.make_async_copy(sent, sent, load_sems.at[0]).wait()
    sent = message.at[pl.ds(0, N_MEM - 1)]
    pltpu.make_async_copy(sent, sent, obs_send).wait()
    for c in range(CHUNKS):
        sent = rows_in.at[c, pl.ds(0, N_MEM - 1)]
        pltpu.make_async_copy(sent, sent, in_send.at[c]).wait()
        pltpu.make_async_copy(sent, sent, out_send.at[c]).wait()
        pltpu.make_async_copy(rows_out.at[c], rows_out.at[c], out_recv.at[c]).wait()


def finish(rows, parts, out, load_out, load_v, sems):
    rows_copy = pltpu.make_async_copy(rows, out, sems.at[0])
    rows_copy.start()
    load_v[...] = jnp.sum(parts[...], 0) * (1.0 / (OBS * CAP))
    load_copy = pltpu.make_async_copy(load_v, load_out, sems.at[1])
    load_copy.start()
    rows_copy.wait()
    load_copy.wait()


def per_device(background, obs_value, obs_height, obs_weight, counts, owner, loc_index, loc_table):
    hbm = pl.BlockSpec(memory_space=pl.ANY)

    def keep(x):
        return pltpu.with_memory_space_constraint(x, pltpu.HBM)

    dma = pltpu.SemaphoreType.DMA
    analysis, load = pl.pallas_call(
        kernel,
        out_shape=(
            jax.ShapeDtypeStruct((COLS_T, WIDTH), F32),
            jax.ShapeDtypeStruct((N_TILE, 1, 128), F32),
        ),
        in_specs=[hbm] * 8,
        out_specs=(hbm, hbm),
        scratch_shapes=[
            pltpu.VMEM((OBS_L, COLS_T), F32),
            pltpu.VMEM((OBS_L, COLS_T), F32),
            pltpu.VMEM((OBS_L, COLS_T), F32),
            pltpu.VMEM((OBS_L, COLS_T), jnp.int32),
            pltpu.VMEM((1, COLS_T), jnp.int32),
            pltpu.VMEM((1, COLS_T), jnp.int32),
            pltpu.VMEM((1, LOC_N), F32),
            pltpu.VMEM((N_MEM, 1, WIDTH), F32),
            pltpu.VMEM((N_MEM, 1, WIDTH), F32),
            pltpu.VMEM((3, OWN, OBS), F32),
            pltpu.VMEM((OWN // 2, 3, 64, 128), F32),
            pltpu.VMEM((N_TILE, 1, 128), F32),
            pltpu.VMEM((CHUNKS, N_MEM, CHUNK, WIDTH), F32),
            pltpu.VMEM((CHUNKS, N_MEM, CHUNK, WIDTH), F32),
            pltpu.VMEM((COLS_T, WIDTH), F32),
            pltpu.SemaphoreType.REGULAR,
            dma((7,)),
            dma,
            dma((CHUNKS,)),
            dma((CHUNKS,)),
            dma((CHUNKS,)),
            dma((CHUNKS,)),
            dma,
            dma,
            dma((2,)),
        ],
        compiler_params=pltpu.CompilerParams(
            collective_id=0, has_side_effects=True, vmem_limit_bytes=16 << 20
        ),
    )(
        keep(background),
        keep(obs_value.T),
        keep(obs_height.T),
        keep(obs_weight.T),
        keep(loc_index.T),
        keep(counts.reshape(1, COLS_T)),
        keep(owner.reshape(1, COLS_T)),
        keep(loc_table.reshape(1, LOC_N)),
    )
    analysis, load = pl.pallas_call(
        finish,
        out_shape=(
            jax.ShapeDtypeStruct((COLS_T, WIDTH), F32),
            jax.ShapeDtypeStruct((1, 128), F32),
        ),
        in_specs=[hbm, pl.BlockSpec(memory_space=pltpu.VMEM)],
        out_specs=(hbm, hbm),
        scratch_shapes=[pltpu.VMEM((1, 128), F32), dma((2,))],
        compiler_params=pltpu.CompilerParams(vmem_limit_bytes=16 << 20),
    )(analysis, load)
    return analysis, load[0, :1]


def solution(mesh):
    placed = (
        P("tile", "mem"),
        P("tile", "mem"),
        P("tile", "mem"),
        P("tile", "mem"),
        P("tile"),
        P("tile", None),
        P("tile", "mem"),
        P(),
    )
    return jax.shard_map(
        per_device,
        mesh=mesh,
        in_specs=placed,
        out_specs=(P("tile", "mem"), P(("mem", "tile"))),
        check_vma=False,
    )
```

```python
import functools

import jax
import jax.numpy as jnp
from jax import lax
from jax.experimental import pallas as pl
from jax.experimental.pallas import tpu as pltpu
from jax.sharding import PartitionSpec as P

LEV = 64
OBS = 128
LOC_N = 16
CAP = 8
N_MEM = 32
N_TILE = 4
COLS_T = 512
OWN = COLS_T // N_MEM
CHUNK = 8
CHUNKS = OWN // CHUNK
OBS_L = OBS // N_MEM
WIDTH = 256
BY_START = [
    2 * chip + core
    for chip in sorted(range(N_MEM // 2), key=lambda k: 1.1 * (k // 4) + 0.45 * (k % 4))
    for core in (1, 0)
]

F32 = jnp.float32
BF16 = jnp.bfloat16
MESH = pl.DeviceIdType.MESH


def iota(shape, axis):
    return lax.broadcasted_iota(jnp.int32, shape, axis)


def split(x):
    high = x.astype(BF16)
    return high, (x - high.astype(F32)).astype(BF16)


def right_side(x, keep0, keep1):
    high, low = split(x)
    top = jnp.concatenate([high * keep0, low * keep0], 1)
    bottom = jnp.concatenate([high * keep1, low * keep1], 1)
    return jnp.concatenate([top, bottom, top, bottom], 0)


def product(a, right):
    high, low = split(a)
    both = jnp.dot(jnp.concatenate([high, low], 1), right, preferred_element_type=F32)
    return both[:, :128] + both[:, 128:]


def lane_masks():
    lane = iota((64, 128), 1)
    left = lane < 64
    keep0 = jnp.where(left, 1.0, 0.0).astype(BF16)
    keep1 = jnp.where(left, 0.0, 1.0).astype(BF16)
    return lane, iota((64, 128), 0), left, keep0, keep1


def observe(fields, shared):
    left = lane_masks()[2]
    level = iota((64, 128), 0).astype(F32)

    def pair(q, carry):
        both = []
        for j in (0, 1):
            value, height, weight = [fields[f, pl.ds(2 * q + j, 1), :] for f in range(3)]
            hat = jnp.maximum(0.0, 1.0 - jnp.abs(level - height))
            hat_next = jnp.maximum(0.0, 1.0 - jnp.abs((level + 1.0) - height))
            weighted = weight * hat
            terms = (weighted * hat, weighted * hat_next, weighted * value)
            both.append([jnp.sum(x, 1, keepdims=True) for x in terms])
        for k in range(3):
            shared[q, k] = jnp.where(left, both[0][k], both[1][k])
        return carry

    lax.fori_loop(0, OWN // 2, pair, 0)


def analyse(blocks, shared):
    lane, row, left, keep0, keep1 = lane_masks()
    left1 = left[:1]
    eye = jnp.where((lane & 63) == row, 1.0, 0.0)
    pairs = range(len(shared))

    def exchange(x, y):
        return jnp.where(left, x, pltpu.roll(y, 64, 1)), jnp.where(left, pltpu.roll(x, 64, 1), y)

    halves, centre, square, mean_col = [], [], [], []
    for q in pairs:
        x, y = [jnp.concatenate([b[:, :128], b[:, 128:]], 0) for b in blocks[2 * q : 2 * q + 2]]
        x = jnp.concatenate(exchange(x, y), 0)
        mean = jnp.sum(x, 0, keepdims=True) * (1.0 / 128.0)
        high, low = split(x - mean)
        both = lax.dot_general(
            jnp.concatenate([high, low], 0),
            jnp.concatenate([jnp.concatenate([high, low], 1)] * 2, 0),
            (((0,), (0,)), ((), ())),
            preferred_element_type=F32,
        )
        square.append(both[:, :128] + both[:, 128:])
        diagonal = eye * mean
        mean_col.append(
            jnp.where(
                left,
                jnp.sum(jnp.where(left, diagonal, 0.0), 1, keepdims=True),
                jnp.sum(jnp.where(left, 0.0, diagonal), 1, keepdims=True),
            )
        )
        halves.append(jnp.concatenate([high, low], 1))
        centre.append(mean)
    base, force = [], []
    for q in pairs:
        g = jnp.where(left, square[q][:64], square[q][64:])
        d, e, w = shared[q]

        def tridiagonal(m):
            return d * m + pltpu.roll(e * m, 1, 0) + e * pltpu.roll(m, 63, 0)

        w = w - tridiagonal(mean_col[q])
        base.append(tridiagonal(g))
        force.append(jnp.broadcast_to(jnp.sum(w * g, 0, keepdims=True), (16, 128)))
    right = [right_side(b, keep0, keep1) for b in base]
    out = [product(jnp.concatenate([base[q], force[q]], 0), right[q]) for q in pairs]
    cube = [product(out[q][:64], right[q]) for q in pairs]
    p, z, t, inverse = [], [], [], []
    for q in pairs:
        b, b2 = base[q], out[q][:64]
        trace = jnp.sum(eye * (254.0 * b + b2), 0, keepdims=True)
        norm2 = 127.0 * 127.0 * 128.0 + jnp.where(
            left1,
            jnp.sum(jnp.where(left1, trace, 0.0), 1, keepdims=True),
            jnp.sum(jnp.where(left1, 0.0, trace), 1, keepdims=True),
        )
        a = lax.rsqrt(norm2)
        u = 127.0 * a
        p.append(
            (u * (2.25 + u * (-1.5 + 0.25 * u))) * eye
            + (a * (2.25 + u * (-3.0 + 0.75 * u))) * b
            + (a * a * (-1.5 + 0.75 * u)) * b2
            + (a * a * a * 0.25) * cube[q]
        )
        z.append((1.5 - 0.5 * u) * eye - (0.5 * a) * b)
        t.append((1.5 - 0.5 * u) * force[q] - (0.5 * a) * out[q][64:])
        inverse.append(a)
    for sweep in range(3):
        right = [right_side(p[q], keep0, keep1) for q in pairs]
        out = [product(jnp.concatenate([p[q], z[q], t[q]], 0), right[q]) for q in pairs]
        cube = [product(out[q][:64], right[q]) for q in pairs]
        for q in pairs:
            z[q] = 1.5 * z[q] - 0.5 * out[q][64:128]
            t[q] = 1.5 * t[q] - 0.5 * out[q][128:]
            p[q] = 2.25 * p[q] - 1.5 * out[q][:64] + 0.25 * cube[q]
    results = []
    for q in pairs:
        out = product(jnp.concatenate([z[q], t[q]], 0), right_side(p[q], keep0, keep1))
        z[q] = 1.5 * z[q] - 0.5 * out[:64]
        t[q] = 1.5 * t[q] - 0.5 * out[64:]
    for q in pairs:
        t_halves = jnp.concatenate(split(t[q]), 1)
        both = jnp.dot(
            jnp.concatenate([halves[q], t_halves], 0),
            right_side(z[q], keep0, keep1),
            preferred_element_type=F32,
        )
        both = both[:, :128] + both[:, 128:]
        full = (centre[q] + inverse[q] * both[128:129]) + jnp.sqrt(127.0 * inverse[q]) * both[:128]
        for x in exchange(full[:64], full[64:]):
            results.append(jnp.concatenate([x[:32], x[32:]], 1))
    return results


def swap_blocks(x):
    row = iota(x.shape, 0)
    block = iota(x.shape, 1) // 16
    for s in (1, 2, 4):
        row_bit = (row // s) % 2
        block_bit = (block // s) % 2
        up = pltpu.roll(pltpu.roll(x, 64 - s, 0), 16 * s, 1)
        down = pltpu.roll(pltpu.roll(x, s, 0), 128 - 16 * s, 1)
        x = jnp.where(row_bit == block_bit, x, jnp.where(row_bit < block_bit, up, down))
    return x


def offsets():
    every = [(z, x, c) for z in range(4) for x in range(4) for c in range(2) if z or x or c]
    return sorted(every, key=lambda o: (-(min(o[0], 4 - o[0]) + min(o[1], 4 - o[1])), o[2]))


def kernel(
    bg, value, height, obs_weight, index, counts, owner, table, out, load_recv,
    value_v, height_v, weight_v, index_v, counts_v, owner_v, table_v,
    message, received, fields, shared, load_send, rows_in, rows_out, rows_own,
    tile_ready, small_sem, stage_sem, in_send, in_recv, out_send, out_recv, obs_send, obs_recv, load_sems,
):
    me = lax.axis_index("mem")
    tile = lax.axis_index("tile")
    z, x, core = me // 8, (me // 2) % 4, me % 2
    zs = [lax.rem(z + d, 4) * 8 for d in range(4)]
    xs = [lax.rem(x + d, 4) * 2 for d in range(4)]
    cores = [core, 1 - core]
    partners = []
    for dz, dx, dc in offsets():
        chips = jnp.where(core == 0, zs[dz] + xs[dx], zs[-dx % 4] + xs[-dz % 4])
        partners.append(chips + cores[dc])
    tile_partners = [lax.rem(tile + d, N_TILE) for d in range(1, N_TILE)]
    small = [
        pltpu.make_async_copy(a, b, small_sem.at[i])
        for i, (a, b) in enumerate(
            zip(
                (value, height, obs_weight, index, counts, owner, table),
                (value_v, height_v, weight_v, index_v, counts_v, owner_v, table_v),
            )
        )
    ]
    for copy in small:
        copy.start()
    stage = pltpu.make_async_copy(bg, rows_own, stage_sem)
    stage.start()
    barrier = pltpu.get_barrier_semaphore()
    for p in partners:
        pl.semaphore_signal(barrier, inc=1, device_id=(p, tile), device_id_type=MESH)

    def greet(there, semaphore, q):
        @pl.when(there)
        def _():
            pl.semaphore_signal(semaphore, inc=1, device_id=(me, q), device_id_type=MESH)

    for q in tile_partners:
        greet(q > tile, barrier, q)
    for copy in small:
        copy.wait()

    localised = jnp.zeros((OBS_L, COLS_T), F32)
    entry = index_v[...]
    table_row = table_v[...]
    for k in range(LOC_N):
        localised = jnp.where(entry == k, table_row[:, k : k + 1], localised)
    live = (me * OBS_L + iota((OBS_L, COLS_T), 0)) < counts_v[...]
    weights = jnp.where(live, localised * weight_v[...], 0.0)
    first = jnp.concatenate([value_v[...], height_v[...]], 0)
    second = jnp.concatenate([weights, jnp.zeros((OBS_L, COLS_T), F32)], 0)
    stack = []
    for b in range(4):
        stack += [first[:, 128 * b : 128 * b + 128], second[:, 128 * b : 128 * b + 128]]
    stack = swap_blocks(jnp.concatenate(stack, 0))
    column_load = jnp.sum(weights, 0, keepdims=True)
    right_half = jnp.concatenate([stack[16 * b + 8 : 16 * b + 16] for b in range(4)], 0)
    lane = iota((N_MEM, 128), 1)
    first_owner = iota((N_MEM, COLS_T), 0) * N_TILE
    owners = owner_v[...]
    for q in range(N_TILE):
        part = jnp.sum(
            jnp.where(first_owner + q == owners, column_load, 0.0), 1, keepdims=True
        )
        right_half = jnp.where(lane == 64 + q, part, right_half)
    left_half = jnp.concatenate([stack[16 * b : 16 * b + 8] for b in range(4)], 0)
    message[...] = jnp.concatenate([left_half, right_half], 1).reshape(N_MEM, 1, WIDTH)

    def source(c, p):
        return rows_own.at[pl.ds(pl.multiple_of(p * OWN + c * CHUNK, CHUNK), CHUNK)]

    stage.wait()
    for c in range(CHUNKS):
        pltpu.make_async_copy(source(c, me), rows_in.at[c, me], in_recv.at[c]).start()
    pl.semaphore_wait(barrier, N_MEM - 1 + tile)

    def send_rows(c):
        for p in partners:
            pltpu.make_async_remote_copy(
                src_ref=source(c, p),
                dst_ref=rows_in.at[c, me],
                send_sem=in_send.at[c],
                recv_sem=in_recv.at[c],
                device_id=(p, tile),
                device_id_type=MESH,
            ).start()

    for p in partners:
        pltpu.make_async_remote_copy(
            src_ref=message.at[p],
            dst_ref=received.at[me],
            send_sem=obs_send,
            recv_sem=obs_recv,
            device_id=(p, tile),
            device_id_type=MESH,
        ).start()
    pltpu.make_async_copy(message.at[me], received.at[me], obs_recv).start()
    for c in range(CHUNKS):
        send_rows(c)

    for q in tile_partners:
        greet(q < tile, tile_ready, q)
    pltpu.make_async_copy(received, received, obs_recv).wait()
    arrived = received[...].reshape(N_MEM, WIDTH)
    arrived = arrived.T
    for f in range(3):
        fields[f] = jnp.concatenate(
            [arrived[(4 * f + o) * OWN : (4 * f + o + 1) * OWN, :N_MEM] for o in range(OBS_L)], 1
        )
    loads = jnp.sum(arrived[192 : 192 + N_TILE], 1, keepdims=True)
    load_send[...] = jnp.broadcast_to(loads, (N_TILE, 128)).reshape(N_TILE, 1, 128)

    @pl.when(tile < N_TILE - 1)
    def _():
        pl.semaphore_wait(tile_ready, N_TILE - 1 - tile)

    for q in tile_partners:
        pltpu.make_async_remote_copy(
            src_ref=load_send.at[q],
            dst_ref=load_recv.at[tile],
            send_sem=load_sems.at[0],
            recv_sem=load_sems.at[1],
            device_id=(me, q),
            device_id_type=MESH,
        ).start()
    pltpu.make_async_copy(load_send.at[tile], load_recv.at[tile], load_sems.at[1]).start()

    observe(fields, shared)

    def step(c, carry):
        pltpu.make_async_copy(rows_in.at[c], rows_in.at[c], in_recv.at[c]).wait()
        results = analyse(
            [rows_in[c, :, i, :] for i in range(CHUNK)],
            [
                [shared[c * (CHUNK // 2) + q, k] for k in range(3)]
                for q in range(CHUNK // 2)
            ],
        )
        for i in range(CHUNK):
            rows_out[c, :, i, :] = results[i]
        target = out.at[pl.ds(pl.multiple_of(me * OWN + c * CHUNK, CHUNK), CHUNK)]

        def send_out(p):
            pltpu.make_async_remote_copy(
                src_ref=rows_out.at[c, p],
                dst_ref=target,
                send_sem=out_send.at[c],
                recv_sem=out_recv.at[c],
                device_id=(p, tile),
                device_id_type=MESH,
            ).start()

        for p in BY_START:
            pl.when(p != me)(functools.partial(send_out, p))
        pltpu.make_async_copy(rows_out.at[c, me], target, out_recv.at[c]).start()
        return carry

    lax.fori_loop(0, CHUNKS, step, 0)

    pltpu.make_async_copy(load_recv, load_recv, load_sems.at[1]).wait()
    sent = load_send.at[pl.ds(0, N_TILE - 1)]
    pltpu.make_async_copy(sent, sent, load_sems.at[0]).wait()
    sent = message.at[pl.ds(0, N_MEM - 1)]
    pltpu.make_async_copy(sent, sent, obs_send).wait()
    for c in range(CHUNKS):
        sent = rows_in.at[c, pl.ds(0, N_MEM - 1)]
        pltpu.make_async_copy(sent, sent, in_send.at[c]).wait()
        pltpu.make_async_copy(sent, sent, out_send.at[c]).wait()
        pltpu.make_async_copy(rows_out.at[c], rows_out.at[c], out_recv.at[c]).wait()


def finish(rows, parts, out, load_out, load_v, sems):
    rows_copy = pltpu.make_async_copy(rows, out, sems.at[0])
    rows_copy.start()
    load_v[...] = jnp.sum(parts[...], 0) * (1.0 / (OBS * CAP))
    load_copy = pltpu.make_async_copy(load_v, load_out, sems.at[1])
    load_copy.start()
    rows_copy.wait()
    load_copy.wait()


def per_device(background, obs_value, obs_height, obs_weight, counts, owner, loc_index, loc_table):
    hbm = pl.BlockSpec(memory_space=pl.ANY)

    def keep(x):
        return pltpu.with_memory_space_constraint(x, pltpu.HBM)

    dma = pltpu.SemaphoreType.DMA
    analysis, load = pl.pallas_call(
        kernel,
        out_shape=(
            jax.ShapeDtypeStruct((COLS_T, WIDTH), F32),
            jax.ShapeDtypeStruct((N_TILE, 1, 128), F32),
        ),
        in_specs=[hbm] * 8,
        out_specs=(hbm, hbm),
        scratch_shapes=[
            pltpu.VMEM((OBS_L, COLS_T), F32),
            pltpu.VMEM((OBS_L, COLS_T), F32),
            pltpu.VMEM((OBS_L, COLS_T), F32),
            pltpu.VMEM((OBS_L, COLS_T), jnp.int32),
            pltpu.VMEM((1, COLS_T), jnp.int32),
            pltpu.VMEM((1, COLS_T), jnp.int32),
            pltpu.VMEM((1, LOC_N), F32),
            pltpu.VMEM((N_MEM, 1, WIDTH), F32),
            pltpu.VMEM((N_MEM, 1, WIDTH), F32),
            pltpu.VMEM((3, OWN, OBS), F32),
            pltpu.VMEM((OWN // 2, 3, 64, 128), F32),
            pltpu.VMEM((N_TILE, 1, 128), F32),
            pltpu.VMEM((CHUNKS, N_MEM, CHUNK, WIDTH), F32),
            pltpu.VMEM((CHUNKS, N_MEM, CHUNK, WIDTH), F32),
            pltpu.VMEM((COLS_T, WIDTH), F32),
            pltpu.SemaphoreType.REGULAR,
            dma((7,)),
            dma,
            dma((CHUNKS,)),
            dma((CHUNKS,)),
            dma((CHUNKS,)),
            dma((CHUNKS,)),
            dma,
            dma,
            dma((2,)),
        ],
        compiler_params=pltpu.CompilerParams(
            collective_id=0, has_side_effects=True, vmem_limit_bytes=16 << 20
        ),
    )(
        keep(background),
        keep(obs_value.T),
        keep(obs_height.T),
        keep(obs_weight.T),
        keep(loc_index.T),
        keep(counts.reshape(1, COLS_T)),
        keep(owner.reshape(1, COLS_T)),
        keep(loc_table.reshape(1, LOC_N)),
    )
    analysis, load = pl.pallas_call(
        finish,
        out_shape=(
            jax.ShapeDtypeStruct((COLS_T, WIDTH), F32),
            jax.ShapeDtypeStruct((1, 128), F32),
        ),
        in_specs=[hbm, pl.BlockSpec(memory_space=pltpu.VMEM)],
        out_specs=(hbm, hbm),
        scratch_shapes=[pltpu.VMEM((1, 128), F32), dma((2,))],
        compiler_params=pltpu.CompilerParams(vmem_limit_bytes=16 << 20),
    )(analysis, load)
    return analysis, load[0, :1]


def solution(mesh):
    placed = (
        P("tile", "mem"),
        P("tile", "mem"),
        P("tile", "mem"),
        P("tile", "mem"),
        P("tile"),
        P("tile", None),
        P("tile", "mem"),
        P(),
    )
    return jax.shard_map(
        per_device,
        mesh=mesh,
        in_specs=placed,
        out_specs=(P("tile", "mem"), P(("mem", "tile"))),
        check_vma=False,
    )
```
